128 devices in a mesh: lat: 16 (over y_hi, x, core), lon: 8 (over y_lo, z).
Axes of the slice: x: 4, y: 4 (y_hi: 2, y_lo: 2; y = y_hi * 2 + y_lo), z: 4, core: 2. Of those that a mesh axis runs over, the one named last changes fastest.
Arguments:
- ensemble: float32 [2, 1, 2048, 16384], P(None, None, 'lat', 'lon'), may hold values from -6 to 6
- cross_mix: float32 [2, 2048, 16384], P(None, 'lat', 'lon'), may hold values from -0.5 to 0.5
- sea_mask: int32 [2048, 16384], P('lat', 'lon'), may hold values 0 or 1
- level_rates: float32 [2, 2], replicated, may hold values from 1 to 256, as said below
- panel_inverse: float32 [2, 2, 128, 128], replicated, may hold values from 0 to 1, as said below
- reduced_lon: float32 [2, 256, 256], replicated, as said below
- reduced_lat: float32 [2, 32, 32], replicated, as said below
Outputs:
- smoothed: float32 [2, 1, 2048, 16384], P(None, None, 'lat', 'lon')
The draws below stay inside these ranges and needn't reach their ends.
Inputs may be any that keep to these rules, and one draw needn't show every extreme that they name: `level_rates`: the same for every point of a level. `panel_inverse`: the inverse of the 128 x 128 tridiagonal matrix whose diagonal entries are one plus twice a (that is 1 + 2*a) and whose entries beside the diagonal are -a, a taken from level_rates. `reduced_lon`: the inverse of the system that the longitude line solve's panel end values satisfy, for the given panel inverses and rates. `reduced_lat`: the inverse of the system that the latitude line solve's panel end values satisfy, for the given panel inverses and rates.
All inputs are finite; a program needn't handle non-finite values. No bound on the sum of `sea_mask` on one device may be relied on, other than what follows from the above.
Results may differ from the reference program's by a relative error of at most 0.00018.
Values sent between devices are 32-bit elements; how exact they have to be, the bound alone decides.
No kernel may reach another device: no remote copies, remote signals or barrier semaphores. Data moves between devices by JAX's collectives and lax.ppermute only.
A program may use at most 128 MiB of HBM per device.

```python
import math
import jax
import jax.numpy as jnp
from jax import lax

PANEL = 128
LEV = 2
SAMP = 1
STEPS = 2
NLAT = 2048
NLON = 16384


def rate_table(key):
    return jnp.exp(jax.random.uniform(jax.random.fold_in(key, 11), (2, LEV), jnp.float32, 0.0, math.log(256.0)))


def panel_inverses(rates):
    eye_panel = jnp.eye(PANEL, dtype=jnp.float32)
    beside = jnp.eye(PANEL, k=1, dtype=jnp.float32) + jnp.eye(PANEL, k=-1, dtype=jnp.float32)
    matrices = (1.0 + 2.0 * rates)[..., None, None] * eye_panel - rates[..., None, None] * beside
    return jnp.linalg.inv(matrices)


def unit_pair(row_slot, col_slot):
    return jnp.zeros((2, 2), jnp.float32).at[row_slot, col_slot].set(1.0)


def coupling(coefficient, onehot, row_slot, col_slot):
    return coefficient[:, None, None, None, None] * onehot[None, :, None, :, None] * unit_pair(row_slot, col_slot)[None, None, :, None, :]


def reduced_inverse(inverse, rates, count, periodic):
    index_row = jnp.arange(count)
    prev_onehot = (((index_row - 1) % count)[:, None] == index_row[None, :]).astype(jnp.float32)
    next_onehot = (((index_row + 1) % count)[:, None] == index_row[None, :]).astype(jnp.float32)
    if not periodic:
        prev_onehot = prev_onehot * (index_row > 0)[:, None].astype(jnp.float32)
        next_onehot = next_onehot * (index_row < count - 1)[:, None].astype(jnp.float32)
    panel = inverse.shape[-1]
    couple = coupling(inverse[:, 0, 0], prev_onehot, 0, 1) + coupling(inverse[:, 0, panel - 1], next_onehot, 0, 0)
    couple = couple + coupling(inverse[:, panel - 1, 0], prev_onehot, 1, 1) + coupling(inverse[:, panel - 1, panel - 1], next_onehot, 1, 0)
    system = jnp.eye(2 * count, dtype=jnp.float32) - rates[:, None, None] * couple.reshape((LEV, 2 * count, 2 * count))
    return jnp.linalg.inv(system)


def draw_level_rates(key, part):
    return rate_table(key)


def draw_panel_inverse(key, part):
    return panel_inverses(rate_table(key))


def draw_reduced_lon(key, part):
    rates = rate_table(key)
    return reduced_inverse(panel_inverses(rates)[0], rates[0], NLON // PANEL, True)


def draw_reduced_lat(key, part):
    rates = rate_table(key)
    return reduced_inverse(panel_inverses(rates)[1], rates[1], NLAT // PANEL, False)


def plant(values, own_key, least, largest):
    longest = values.shape.index(max(values.shape))
    spots = []
    for shift in (0, 1):
        where = [jax.random.randint(jax.random.fold_in(own_key, axis), (), 0, length) for axis, length in enumerate(values.shape)]
        where[longest] = (where[longest] + shift) % values.shape[longest]
        spots.append(tuple(where))
    return values.at[spots[0]].set(least).at[spots[1]].set(largest)


def steps_of(rng, extent, cuts, smallest, high):
    gain = 1.0
    for position, parts in cuts:
        draws = jax.random.uniform(jax.random.fold_in(jax.random.fold_in(rng, 6), position), (parts,), jnp.float32, smallest / len(cuts), high / len(cuts))
        gain = gain * jnp.repeat(jnp.exp(draws), extent[position] // parts).reshape((-1,) + (1,) * (len(extent) - 1 - position))
    return gain


def scatter_about(stream_key, shape, deviation, most, cuts=(), kind=jnp.bfloat16):
    loudness = steps_of(stream_key, shape, cuts, -0.22, 0.18) if cuts else 1.0
    array = jax.random.normal(stream_key, shape, jnp.float32) * deviation * loudness
    return jnp.minimum(jnp.maximum(array, -most), most).astype(kind)


def setup_inputs(seed: int = 0) -> dict:
    key_of = jax.random.split(jax.random.key(seed), 8)
    return {
        "ensemble": scatter_about(key_of[0], (LEV, SAMP, NLAT, NLON), 1.0, 6.0, ((2, 16), (3, 8)), jnp.float32),
        "cross_mix": jnp.clip(jax.random.uniform(key_of[1], (LEV, NLAT, NLON), jnp.float32, -0.5, 0.5) * steps_of(key_of[1], (LEV, NLAT, NLON), ((1, 16), (2, 8)), -0.4, 0.0), -0.5, 0.5),
        "sea_mask": plant((jax.random.randint(key_of[2], (NLAT, NLON), 0, 4) < 3).astype(jnp.int32), jax.random.fold_in(key_of[2], 1), 0, 1),
        "level_rates": draw_level_rates(jax.random.fold_in(key_of[7], 71), 0),
        "panel_inverse": draw_panel_inverse(jax.random.fold_in(key_of[7], 71), 0),
        "reduced_lon": draw_reduced_lon(jax.random.fold_in(key_of[7], 71), 0),
        "reduced_lat": draw_reduced_lat(jax.random.fold_in(key_of[7], 71), 0),
    }


highest = lax.Precision.HIGHEST

def cross_term(extended):
    return extended[:, :, 2:, 2:] - extended[:, :, 2:, :-2] - extended[:, :, :-2, 2:] + extended[:, :, :-2, :-2]

def explicit_terms(extended):
    centre = extended[:, :, 1:-1, 1:-1]
    along_lon = extended[:, :, 1:-1, 2:] - 2.0 * centre + extended[:, :, 1:-1, :-2]
    along_lat = extended[:, :, 2:, 1:-1] - 2.0 * centre + extended[:, :, :-2, 1:-1]
    return (along_lon, along_lat, cross_term(extended))

def lon_panels(values, inverse):
    panel = inverse.shape[1]
    dims = values.shape
    split = values.reshape(dims[:3] + (dims[3] // panel, panel))
    return jnp.einsum('lsrcq,lpq->lsrcp', split, inverse, precision=highest)

def lon_ends(solved):
    paired = jnp.stack((solved[..., 0], solved[..., -1]), axis=-1)
    return paired.reshape(paired.shape[:3] + (-1,))

def lon_finish(solved, prev_last, next_first, inverse, rate_lon):
    left_col = inverse[:, None, None, None, :, 0]
    right_col = inverse[:, None, None, None, :, -1]
    scale = rate_lon[:, None, None, None, None]
    result = solved + scale * (prev_last[..., None] * left_col + next_first[..., None] * right_col)
    return result.reshape(result.shape[:3] + (-1,))

def lon_solve(values, inverse, reduced, rate_lon):
    solved = lon_panels(values, inverse)
    bounds = jnp.einsum('lsrk,lmk->lsrm', lon_ends(solved), reduced, precision=highest)
    pairs = bounds.reshape(bounds.shape[:3] + (-1, 2))
    prev_last = jnp.roll(pairs[..., 1], 1, axis=-1)
    next_first = jnp.roll(pairs[..., 0], -1, axis=-1)
    return lon_finish(solved, prev_last, next_first, inverse, rate_lon)

def lat_panels(values, inverse):
    panel = inverse.shape[1]
    dims = values.shape
    split = values.reshape((dims[0], dims[1], dims[2] // panel, panel, dims[3]))
    return jnp.einsum('lscqw,lpq->lscpw', split, inverse, precision=highest)

def lat_ends(solved):
    paired = jnp.stack((solved[:, :, :, 0, :], solved[:, :, :, -1, :]), axis=3)
    return paired.reshape((paired.shape[0], paired.shape[1], -1, paired.shape[4]))

def lat_shifted(pairs):
    first_end = pairs[:, :, :, 0, :]
    last_end = pairs[:, :, :, 1, :]
    zero_row = jnp.zeros_like(last_end[:, :, :1])
    prev_last = jnp.concatenate((zero_row, last_end[:, :, :-1]), axis=2)
    next_first = jnp.concatenate((first_end[:, :, 1:], zero_row), axis=2)
    return (prev_last, next_first)

def lat_finish(solved, prev_last, next_first, inverse, rate_lat):
    left_col = inverse[:, None, None, :, 0][..., None]
    right_col = inverse[:, None, None, :, -1][..., None]
    scale = rate_lat[:, None, None, None, None]
    result = solved + scale * (prev_last[:, :, :, None, :] * left_col + next_first[:, :, :, None, :] * right_col)
    dims = result.shape
    return result.reshape((dims[0], dims[1], dims[2] * dims[3], dims[4]))

def lat_solve(values, inverse, reduced, rate_lat):
    solved = lat_panels(values, inverse)
    bounds = jnp.einsum('lskw,lmk->lsmw', lat_ends(solved), reduced, precision=highest)
    dims = bounds.shape
    pairs = bounds.reshape((dims[0], dims[1], -1, 2, dims[3]))
    prev_last, next_first = lat_shifted(pairs)
    return lat_finish(solved, prev_last, next_first, inverse, rate_lat)

def extend_full(values):
    wide = jnp.pad(values, ((0, 0), (0, 0), (0, 0), (1, 1)), mode='wrap')
    return jnp.pad(wide, ((0, 0), (0, 0), (1, 1), (0, 0)))

def reference(ensemble, cross_mix, sea_mask, level_rates, panel_inverse, reduced_lon, reduced_lat):
    sea_float = sea_mask.astype(jnp.float32)[None, None]
    mixing = cross_mix[:, None]
    rate_lon = level_rates[0]
    rate_lat = level_rates[1]
    scale_lon = rate_lon[:, None, None, None]
    scale_lat = rate_lat[:, None, None, None]
    current = ensemble
    for repeat in range(STEPS):
        along_lon, along_lat, diagonal_diff = explicit_terms(extend_full(current))
        start_value = sea_float * (current + mixing * diagonal_diff + 2.0 * scale_lon * along_lon + 2.0 * scale_lat * along_lat)
        first_lon = lon_solve(start_value - scale_lon * along_lon, panel_inverse[0], reduced_lon, rate_lon)
        first_lat = lat_solve(first_lon - scale_lat * along_lat, panel_inverse[1], reduced_lat, rate_lat)
        correction = cross_term(extend_full(first_lat - current))
        corrected = start_value + 0.5 * mixing * correction
        second_lon = lon_solve(corrected - scale_lon * along_lon, panel_inverse[0], reduced_lon, rate_lon)
        second_lat = lat_solve(second_lon - scale_lat * along_lat, panel_inverse[1], reduced_lat, rate_lat)
        current = sea_float * second_lat
    return current
```

```python
import functools

import jax
import jax.numpy as jnp
from jax import lax
from jax.experimental import pallas as pl
from jax.experimental.pallas import tpu as pltpu
from jax.sharding import PartitionSpec as P

LEV, ROWS, COLS = 2, 128, 2048
KT, TT, SS, LN = 16, 16, 8, 128
NLAT_DEV, NLON_DEV = 16, 8
NLAT, NLON = ROWS * NLAT_DEV, COLS * NLON_DEV
F32, BF16 = jnp.float32, jnp.bfloat16
VM = pl.BlockSpec(memory_space=pltpu.VMEM)
SM = pl.BlockSpec(memory_space=pltpu.SMEM)
HB = pl.BlockSpec(memory_space=pl.ANY)
PARAMS = pltpu.CompilerParams(vmem_limit_bytes=40 * 1024 * 1024)

L_P, L_LQ, L_Q, L_CQ, L_CQL, L_CP, L_GQ, L_GP = range(8)
PK = 40


def shape(*dims, dtype=F32):
    return jax.ShapeDtypeStruct(dims, dtype)


def iota(dims, axis):
    return lax.broadcasted_iota(jnp.int32, dims, axis)


def fiota(dims, axis):
    return iota(dims, axis).astype(F32)


class Rates:
    def __init__(self, par, level):
        self.t1, self.t2, self.a1, self.a2, self.c1, self.c2 = (par[8 * level + i] for i in range(6))


def position(par):
    return par[16], par[17]


def split3(x):
    high = x.astype(BF16)
    rest = x - high.astype(F32)
    mid = rest.astype(BF16)
    return high, mid, (rest - mid.astype(F32)).astype(BF16)


def dot(x, y):
    return jnp.dot(x, y, preferred_element_type=F32)


def tables_kernel(par, u_hbm, m_hbm, k_hbm, ul, ml, kl, w1, w3, k1, k3, et, lt, el, su, sm, sk, sem):
    copies = []
    for l in range(LEV):
        copies.append([pltpu.make_async_copy(u_hbm.at[l, :, pl.ds(k * LN, LN)], su.at[l, k], sem.at[l]) for k in range(KT)])
    for l in range(LEV):
        copies.append([pltpu.make_async_copy(m_hbm.at[l, :, pl.ds(k * LN, LN)], sm.at[l, k], sem.at[2 + l]) for k in range(KT)])
    copies.append([pltpu.make_async_copy(k_hbm.at[:, pl.ds(k * LN, LN)], sk.at[k], sem.at[4]) for k in range(KT)])
    for group in copies:
        for c in group:
            c.start()
    i_pos, _ = position(par)
    for l in range(LEV):
        r = Rates(par, l)
        dist = jnp.abs(fiota((LN, LN), 0) - fiota((LN, LN), 1))
        high, mid, low = split3(r.c1 * jnp.exp(-r.t1 * dist))
        k1[l] = jnp.concatenate([high, mid], axis=1)
        k3[l] = low
        lane = iota((LN, LN), 1)
        row = fiota((LN, LN), 0)
        slot = lane % 32
        rising = ((lane < 96) & (slot >= 16)) | (lane == 97)
        base = jnp.exp(-r.t1 * jnp.where(rising, row, (LN - 1) - row))

        def weights(k, carry):
            kf = k.astype(F32)
            pick = jnp.where((lane < 96) & (slot % 16 == k), 1.0, 0.0)
            pick = jnp.where(lane == 96, jnp.exp(-r.t1 * (LN * (KT - 1 - kf))), pick)
            pick = jnp.where(lane == 97, jnp.exp(-r.t1 * (LN * kf)), pick)
            high, mid, low = split3(base * pick)
            w1[l, k] = jnp.concatenate([high, mid], axis=1)
            w3[l, k] = low
            return carry

        lax.fori_loop(0, KT, weights, 0)
        slot = iota((32, LN), 0)
        col = fiota((32, LN), 1)
        own = (slot % 16).astype(F32)
        for k in range(KT):
            gap = jnp.where(slot < 16, k - own, own - k)
            power = (gap - 1) * LN + jnp.where(slot < 16, col + 1, LN - col)
            value = jnp.where(gap > 0, r.c1 * jnp.exp(-r.t1 * jnp.maximum(power, 0.0)), 0.0)
            high, mid, low = split3(value)
            zero = jnp.zeros_like(high)
            et[l, :, pl.ds(k * LN, LN)] = jnp.concatenate([high, mid, low, zero, high, mid, high, zero], axis=0)
        lane_f = fiota((SS, LN), 1)
        for k in range(KT):
            el[l, 0, k] = r.c1 * jnp.exp(-r.t1 * (k * LN + lane_f + 1.0))
            el[l, 1, k] = r.c1 * jnp.exp(-r.t1 * (COLS - k * LN - lane_f))
        sub = fiota((SS, LN), 0)
        scale = r.c2 / (1.0 - jnp.exp(jnp.full((SS, LN), -2.0 * (NLAT + 1), F32) * r.t2))
        for t in range(TT):
            local = sub * TT + t
            index = local + i_pos * ROWS
            p = 1.0 - jnp.exp(-2.0 * r.t2 * (index + 1.0))
            q = 1.0 - jnp.exp(-2.0 * r.t2 * (NLAT - index))
            lt[l, L_P, t] = p
            lt[l, L_Q, t] = q
            lt[l, L_LQ, t] = q * jnp.exp(jnp.full((SS, LN), -float(t), F32) * r.t2)
            lt[l, L_CQ, t] = scale * q
            lt[l, L_CQL, t] = scale * q * jnp.exp(jnp.full((SS, LN), -float(t + 1), F32) * r.t2)
            lt[l, L_CP, t] = scale * p
            lt[l, L_GQ, t] = scale * q * jnp.exp(-r.t2 * (local + 1.0))
            lt[l, L_GP, t] = scale * p * jnp.exp(-r.t2 * (ROWS - local))
    for group in copies:
        for c in group:
            c.wait()

    def move(k, carry):
        for t in range(TT):
            for l in range(LEV):
                ul[l, k, t] = su[l, k, pl.ds(t, SS, stride=TT), :]
                ml[l, k, t] = sm[l, k, pl.ds(t, SS, stride=TT), :]
            kl[k, t] = sk[k, pl.ds(t, SS, stride=TT), :].astype(F32)
        return carry

    lax.fori_loop(0, KT, move, 0)


def right_left(tiles, ext):
    lane = iota((1, SS, LN), 2)
    right = pltpu.roll(tiles, LN - 1, 2)
    left = pltpu.roll(tiles, 1, 2)
    if ext is None:
        beyond_right = before_left = jnp.zeros((1, SS, LN), F32)
    else:
        beyond_right = pltpu.roll(ext, LN - 2, 1)[None]
        before_left = ext[None]
    next_right = jnp.concatenate([right[1:], beyond_right], axis=0)
    prev_left = jnp.concatenate([before_left, left[:-1]], axis=0)
    return jnp.where(lane == LN - 1, next_right, right), jnp.where(lane == 0, prev_left, left)


def north_of(last, halo):
    return jnp.where(iota(last.shape, last.ndim - 2) == 0, halo, pltpu.roll(last, 1, last.ndim - 2))


def south_of(first, halo):
    return jnp.where(iota(first.shape, first.ndim - 2) == SS - 1, halo, pltpu.roll(first, SS - 1, first.ndim - 2))


def down_scan(x, t2):
    sub = iota(x.shape, x.ndim - 2)
    x = jnp.where(sub >= 1, pltpu.roll(x, 1, x.ndim - 2), 0.0)
    for step in (1, 2, 4):
        factor = jnp.exp(jnp.full((SS, LN), -float(TT * step), F32) * t2)
        x = x + factor * jnp.where(sub >= step, pltpu.roll(x, step, x.ndim - 2), 0.0)
    return x


def up_scan(x, t2):
    sub = iota(x.shape, x.ndim - 2)
    x = jnp.where(sub < SS - 1, pltpu.roll(x, SS - 1, x.ndim - 2), 0.0)
    for step in (1, 2, 4):
        factor = jnp.exp(jnp.full((SS, LN), -float(TT * step), F32) * t2)
        x = x + factor * jnp.where(sub < SS - step, pltpu.roll(x, SS - step, x.ndim - 2), 0.0)
    return x


def chunk_ends(last, acc, t2):
    carry_down = down_scan(last, t2)
    carry_up = up_scan(acc, t2)
    step = jnp.exp(jnp.full((SS, LN), -float(TT), F32) * t2)
    phi = (last + step * carry_down)[..., SS - 1 : SS, :]
    psi = (acc + step * carry_up)[..., 0:1, :]
    return carry_down, carry_up, jnp.broadcast_to(phi, last.shape), jnp.broadcast_to(psi, last.shape)


def lam2(t2):
    return jnp.exp(jnp.full((SS, LN), -1.0, F32) * t2)


def local_solve(par, qs, xs, ss, w1, w3, k1, k3, et, lt, zl, phi, with_p):
    sums = []
    for l in range(LEV):
        r = Rates(par, l)

        def tile(k, ab):
            high, mid, low = split3(qs[l, k].reshape(ROWS, LN))
            lhs1 = jnp.concatenate([high, mid], axis=1)
            lhs2 = jnp.concatenate([low, high], axis=1)
            kk = k1[l]
            one = dot(lhs1, jnp.concatenate([kk, kk], axis=0))
            two = dot(lhs2, jnp.concatenate([kk[:, :LN], k3[l]], axis=0))
            x = (one[:, :LN] + one[:, LN:] + two).reshape(TT, SS, LN)
            xs[l, k] = xs[l, k] + x if with_p else x
            ww = w1[l, k]
            one = dot(lhs1, jnp.concatenate([ww, ww], axis=0))
            two = dot(lhs2, jnp.concatenate([ww[:, :LN], w3[l, k]], axis=0))
            return ab + (one[:, :LN] + one[:, LN:] + two)

        ab = lax.fori_loop(0, KT, tile, jnp.zeros((ROWS, LN), F32))
        sums.append(ab)
        high, mid, low = split3(ab)
        lane = iota((ROWS, LN), 1)
        second = jnp.where(lane < 64, mid.astype(F32), low.astype(F32)).astype(BF16)
        lhs = jnp.concatenate([high, second], axis=1)
        for k in range(0, KT, 2):
            fix = dot(lhs, et[l, :, pl.ds(k * LN, 2 * LN)])
            xs[l, k] += fix[:, :LN].reshape(TT, SS, LN)
            xs[l, k + 1] += fix[:, LN:].reshape(TT, SS, LN)

        lam = lam2(r.t2)

        def down(t, carry):
            s, acc = carry
            x = xs[l, :, t]
            s = lam * s + lt[l, L_P, t] * x
            ss[:, t] = s
            return s, acc + lt[l, L_LQ, t] * x

        zero = jnp.zeros((KT, SS, LN), F32)
        last, acc = lax.fori_loop(0, TT, down, (zero, zero))
        carry_down, carry_up, phi_l, psi_l = chunk_ends(last, acc, r.t2)
        phi[l, 0] = phi_l
        phi[l, 1] = psi_l

        def up(i, u):
            t = TT - 1 - i
            zl[l, :, t] = lt[l, L_CQ, t] * ss[:, t] + lt[l, L_CQL, t] * carry_down + lt[l, L_CP, t] * u
            return lam * (u + lt[l, L_Q, t] * xs[l, :, t])

        lax.fori_loop(0, TT, up, lam * carry_up)
    return sums


def explicit(r, before, here, after, ext_here, ext_diff, mixing, mask):
    east, west = right_left(here, ext_here)
    lon = east + west - 2.0 * here
    lat = after + before - 2.0 * here
    east, west = right_left(after - before, ext_diff)
    q = mask * (here + mixing * (east - west) + (2.0 * r.a1) * lon + (2.0 * r.a2) * lat) - r.a1 * lon
    return q, -r.a2 * lat


def end_columns(first, last):
    lane = iota((ROWS, LN), 1)
    turned = jnp.where(lane < 64, first, last).T
    return turned[0:1], turned[LN - 1 : LN]


def first_kernel(par, ul, ml, kl, north, south, w1, w3, k1, k3, et, lt, zl, phi, msg, uh, kh, qs, xs, ss):
    def spread(ref, row):
        return jnp.stack([jnp.broadcast_to(ref[row, k : k + 1, :], (SS, LN)) for k in range(KT)])

    for side, ref in ((0, north), (1, south)):
        kh[side, :KT] = spread(ref, 2)
    for l in range(LEV):
        r = Rates(par, l)
        uh[l, 0, :KT] = spread(north, l)
        uh[l, 1, :KT] = spread(south, l)

        def rows(t, before, after):
            q, p = explicit(r, before, ul[l, :, t], after, None, None, ml[l, :, t], kl[:, t])
            qs[l, :, t] = q
            xs[l, :, t] = p

        rows(0, north_of(ul[l, :, TT - 1], uh[l, 0, :KT]), ul[l, :, 1])

        def body(t, carry):
            rows(t, ul[l, :, t - 1], ul[l, :, t + 1])
            return carry

        lax.fori_loop(1, TT - 1, body, 0)
        rows(TT - 1, ul[l, :, TT - 2], south_of(ul[l, :, 0], uh[l, 1, :KT]))
    sums = local_solve(par, qs, xs, ss, w1, w3, k1, k3, et, lt, zl, phi, True)
    parts = []
    for l in range(LEV):
        parts.append(sums[l].T[96:98])
    for l in range(LEV):
        parts.extend(end_columns(ul[l, 0].reshape(ROWS, LN), ul[l, KT - 1].reshape(ROWS, LN)))
    for l in range(LEV):
        parts.extend(end_columns(ml[l, 0].reshape(ROWS, LN), ml[l, KT - 1].reshape(ROWS, LN)))
    parts.extend(end_columns(kl[0].reshape(ROWS, LN), kl[KT - 1].reshape(ROWS, LN)))
    lane = iota((1, LN), 1)
    for row in range(3):
        n0, s0 = north[row, 0:1, :], south[row, 0:1, :]
        n1, s1 = north[row, KT - 1 : KT, :], south[row, KT - 1 : KT, :]
        parts.append(jnp.where(lane == 0, n0, pltpu.roll(s0, 1, 1)))
        parts.append(jnp.where(lane == LN - 1, n1, pltpu.roll(s1, LN - 1, 1)))
    parts.append(jnp.zeros((4, LN), F32))
    block = jnp.concatenate(parts, axis=0)
    for j in range(NLON_DEV):
        msg[j] = block


def row_after(x, halo):
    lane = iota(x.shape, 1)
    y = jnp.where(lane >= LN - SS, pltpu.roll(x, LN - SS - 1, 1), pltpu.roll(x, LN - SS, 1))
    return jnp.where(lane == LN - 1, halo, y)


def row_before(x, halo):
    lane = iota(x.shape, 1)
    y = jnp.where(lane < SS, pltpu.roll(x, SS + 1, 1), pltpu.roll(x, SS, 1))
    return jnp.where(lane == 0, halo, y)


def lane_value(x, index):
    return jnp.sum(jnp.where(iota(x.shape, x.ndim - 1) == index, x, 0.0), axis=-1, keepdims=True)


def as_tile(rows):
    count = sum(r.shape[0] for r in rows)
    return jnp.concatenate(rows + [jnp.zeros((LN - count, LN), F32)], axis=0).T.reshape(TT, SS, LN)


def carry_kernel(first, *refs):
    if first:
        par, got, phi, lt, el, out, pack, ze, ux, kx, uhx, khx = refs
    else:
        par, got, phi, px, lt, el, out, pack, ze = refs
    i_pos, j_pos = position(par)
    peer = fiota((NLON_DEV, LN), 0)
    mine = peer == j_pos
    fluxes = []
    ext = []
    if first:
        kw = pltpu.roll(got[:, 13, :], 1, 0)
        ke = pltpu.roll(got[:, 12, :], NLON_DEV - 1, 0)
        kw_end = pltpu.roll(got[:, 19, :], 1, 0)
        ke_end = pltpu.roll(got[:, 18, :], NLON_DEV - 1, 0)

        def own(x):
            return jnp.sum(jnp.where(mine, x, 0.0), axis=0, keepdims=True)

        def corners(west_end, east_end):
            lane = iota((1, LN), 1)
            w, e = own(west_end), own(east_end)
            w_n, w_s = lane_value(w, LN - 1), lane_value(w, LN - 2)
            e_n, e_s = lane_value(e, 0), lane_value(e, 1)
            pick = lambda a, b: jnp.broadcast_to(jnp.where(lane == 0, a, jnp.where(lane == 1, b, 0.0)), (SS, LN))
            return pick(w_n, e_n), pick(w_s, e_s)

        khx[0], khx[1] = corners(kw_end, ke_end)
        kx[...] = as_tile([own(kw), own(ke)])
    for l in range(LEV):
        r = Rates(par, l)
        a, b = got[:, 2 * l, :], got[:, 2 * l + 1, :]
        one = jnp.full((NLON_DEV, LN), 1.0, F32)
        if first:
            uw = pltpu.roll(got[:, 5 + 2 * l, :], 1, 0)
            ue = pltpu.roll(got[:, 4 + 2 * l, :], NLON_DEV - 1, 0)
            uw_end = pltpu.roll(got[:, 15 + 2 * l, :], 1, 0)
            ue_end = pltpu.roll(got[:, 14 + 2 * l, :], NLON_DEV - 1, 0)
            w_up = row_before(uw, jnp.sum(jnp.where(iota(uw.shape, 1) == LN - 1, uw_end, 0.0), axis=1, keepdims=True))
            w_dn = row_after(uw, jnp.sum(jnp.where(iota(uw.shape, 1) == LN - 2, uw_end, 0.0), axis=1, keepdims=True))
            e_up = row_before(ue, jnp.sum(jnp.where(iota(ue.shape, 1) == 0, ue_end, 0.0), axis=1, keepdims=True))
            e_dn = row_after(ue, jnp.sum(jnp.where(iota(ue.shape, 1) == 1, ue_end, 0.0), axis=1, keepdims=True))
            m0, mn, k0, kn = got[:, 8 + 2 * l, :], got[:, 9 + 2 * l, :], got[:, 12, :], got[:, 13, :]
            h0 = k0 * (m0 * (w_up - w_dn) + 2.0 * r.a1 * uw) - r.a1 * uw
            hn = kn * (mn * (e_dn - e_up) + 2.0 * r.a1 * ue) - r.a1 * ue
            far = jnp.exp(-(COLS - 1.0) * r.t1 * one)
            a = a + far * h0 + hn
            b = b + h0 + far * hn
        whole = 1.0 - jnp.exp(-float(NLON) * r.t1 * one)
        back = j_pos - peer - 1.0
        back = jnp.where(back < 0, back + NLON_DEV, back)
        ahead = peer - j_pos - 1.0
        ahead = jnp.where(ahead < 0, ahead + NLON_DEV, ahead)
        left = jnp.sum(a * (jnp.exp(-r.t1 * COLS * back) / whole), axis=0, keepdims=True)
        right = jnp.sum(b * (jnp.exp(-r.t1 * COLS * ahead) / whole), axis=0, keepdims=True)
        a = jnp.sum(jnp.where(mine, a, 0.0), axis=0, keepdims=True)
        b = jnp.sum(jnp.where(mine, b, 0.0), axis=0, keepdims=True)
        lam = jnp.exp(-r.t1 * jnp.full((1, LN), 1.0, F32))
        far = jnp.exp(-(COLS + 1.0) * r.t1 * jnp.full((1, LN), 1.0, F32))
        xw = r.c1 * (left + lam * b + far * right)
        xe = r.c1 * (right + lam * a + far * left)
        if first:
            pw = -r.a2 * (w_dn + w_up - 2.0 * uw)
            pe = -r.a2 * (e_dn + e_up - 2.0 * ue)
            xw = xw + own(pw)
            xe = xe + own(pe)
            left = left + own(h0) / lam
            right = right + own(hn) / lam
            ux[l] = as_tile([own(uw), own(ue)])
            uhx[l, 0], uhx[l, 1] = corners(uw_end, ue_end)
        x = as_tile([xw, xe, left, right])
        if not first:
            x = x + px[l]
        ext.append(x)
    lams = [lam2(Rates(par, l).t2) for l in range(LEV)]
    zero = jnp.zeros((SS, LN), F32)
    state = [zero, zero]
    acc = [zero, zero]
    kept = [[], []]
    for t in range(TT):
        for l in range(LEV):
            state[l] = lams[l] * state[l] + lt[l, L_P, t] * ext[l][t]
            acc[l] = acc[l] + lt[l, L_LQ, t] * ext[l][t]
            kept[l].append(state[l])
    for l in range(LEV):
        r = Rates(par, l)
        carry_down, carry_up, phi_e, psi_e = chunk_ends(state[l], acc[l], r.t2)
        u = lams[l] * carry_up
        for t in range(TT - 1, -1, -1):
            ze[l, t] = lt[l, L_CQ, t] * kept[l][t] + lt[l, L_CQL, t] * carry_down + lt[l, L_CP, t] * u
            u = lams[l] * (u + lt[l, L_Q, t] * ext[l][t])
        pair = []
        for side, flux in ((0, phi_e), (1, psi_e)):
            tiles = phi[l, side] + lane_value(flux, 2) * el[l, 0] + lane_value(flux, 3) * el[l, 1]
            pair.append([tiles[k] for k in range(KT)] + [flux])
        fluxes.append(pair)
    sub = iota((SS, LN), 0)
    packed = []
    for side in (0, 1):
        rows = fluxes[0][side] + fluxes[1][side]
        rows = rows + [zero] * (PK - len(rows))
        vregs = []
        for v in range(PK // SS):
            y = rows[v * SS]
            for j in range(1, SS):
                y = jnp.where(sub == j, rows[v * SS + j], y)
            vregs.append(y)
        packed.append(jnp.concatenate(vregs, axis=0))
        pack[side] = packed[side]
    t2 = level_rows(Rates(par, 0).t2, Rates(par, 1).t2)
    for p in range(NLAT_DEV):
        away = jnp.maximum(jnp.abs(p - i_pos) - 1.0, 0.0)
        factor = jnp.exp(-(ROWS * away) * t2)
        ahead = jnp.full((PK, LN), p - i_pos, F32) > 0
        out[p] = factor * jnp.where(ahead, packed[0], packed[1])


def level_rows(low, high):
    return jnp.where(iota((PK, LN), 0) <= KT, low, high)


def arrive(par, got, pack, tb, vb, hb):
    i_pos, _ = position(par)
    zero = jnp.zeros((PK, LN), F32)
    above, below = zero, zero
    for p in range(NLAT_DEV):
        side = jnp.full((PK, LN), p - i_pos, F32)
        above = above + jnp.where(side < 0, got[p], 0.0)
        below = below + jnp.where(side > 0, got[p], 0.0)
    t2 = level_rows(Rates(par, 0).t2, Rates(par, 1).t2)
    scale = level_rows(Rates(par, 0).c2, Rates(par, 1).c2) / (1.0 - jnp.exp(-2.0 * (NLAT + 1) * t2))
    lam = jnp.exp(-t2)
    block = jnp.exp(-float(ROWS) * t2)
    start = i_pos * ROWS
    q_n = 1.0 - jnp.exp(-2.0 * t2 * (NLAT + 1.0 - start))
    p_n = 1.0 - jnp.exp(-2.0 * t2 * start)
    q_s = 1.0 - jnp.exp(-2.0 * t2 * (NLAT - ROWS - start))
    p_s = 1.0 - jnp.exp(-2.0 * t2 * (ROWS + 1.0 + start))
    north = scale * (q_n * above + p_n * lam * (pack[1] + block * below))
    south = scale * (q_s * lam * (pack[0] + block * above) + p_s * below)
    for l in range(LEV):
        for k in range(KT + 1):
            at = l * (KT + 1) + k
            wide = lambda x: jnp.broadcast_to(x[at : at + 1], (SS, LN))
            tb[l, k] = wide(above)
            vb[l, k] = wide(below)
            if hb is not None:
                hb[l, 0, k] = wide(north)
                hb[l, 1, k] = wide(south)


def solved_rows(l, t, zl, ze, el, lt, tb, vb):
    extra = ze[l, t]
    gq, gp = lt[l, L_GQ, t], lt[l, L_GP, t]
    z_left = jnp.broadcast_to(extra[:, 2:3], (SS, LN))
    z_right = jnp.broadcast_to(extra[:, 3:4], (SS, LN))
    own = zl[l, :, t] + el[l, 0] * z_left + el[l, 1] * z_right + gq * tb[l, :KT] + gp * vb[l, :KT]
    return own, extra + gq * tb[l, KT] + gp * vb[l, KT]


def send_sums(sums, msg):
    block = jnp.concatenate([s.T[96:98] for s in sums] + [jnp.zeros((4, LN), F32)], axis=0)
    for j in range(NLON_DEV):
        msg[j] = block


def half_kernel(par, got, pack, zl, ze, ul, ux, uh, uhx, ml, el, w1, w3, k1, k3, et, lt,
                y2, yx, yh, zo, phi, msg, px, tb, vb, vs, qs, xs, ss):
    arrive(par, got, pack, tb, vb, yh)
    for l in range(LEV):
        r = Rates(par, l)

        def rows(t, carry):
            own, extra = solved_rows(l, t, zl, ze, el, lt, tb, vb)
            y2[l, :, t] = own
            yx[l, t] = extra
            vs[:KT, t + 1] = own - ul[l, :, t]
            vs[KT, t + 1] = extra - ux[l, t]
            px[l, t] = jnp.zeros((SS, LN), F32)
            return carry

        lax.fori_loop(0, TT, rows, 0)
        for side, edge, at, turn in ((0, TT, 0, north_of), (1, 1, TT + 1, south_of)):
            vs[:KT, at] = turn(vs[:KT, edge], yh[l, side, :KT] - uh[l, side, :KT])
            vs[KT, at] = turn(vs[KT, edge], yh[l, side, KT] - uhx[l, side])

        def body(t, carry):
            diff = vs[:, t + 2] - vs[:, t]
            east, west = right_left(diff[:KT], diff[KT])
            qs[l, :, t] = 0.5 * ml[l, :, t] * (east - west)
            return carry

        lax.fori_loop(0, TT, body, 0)
    send_sums(local_solve(par, qs, xs, ss, w1, w3, k1, k3, et, lt, zo, phi, False), msg)


def step_kernel(par, got, pack, zl, ze, y2, yx, yh, kl, kx, kh, khx, ml, el, w1, w3, k1, k3, et, lt,
                un, unx, unh, unhx, zo, phi, msg, px, tb, vb, hb, vs, qs, xs, ss):
    arrive(par, got, pack, tb, vb, hb)
    for l in range(LEV):
        r = Rates(par, l)

        def rows(t, carry):
            own, extra = solved_rows(l, t, zl, ze, el, lt, tb, vb)
            own = kl[:, t] * (own + y2[l, :, t])
            extra = kx[t] * (extra + yx[l, t])
            un[l, :, t] = own
            unx[l, t] = extra
            vs[:KT, t + 1] = own
            vs[KT, t + 1] = extra
            return carry

        lax.fori_loop(0, TT, rows, 0)
        for side, edge, at, turn in ((0, TT, 0, north_of), (1, 1, TT + 1, south_of)):
            halo = kh[side, :KT] * (yh[l, side, :KT] + hb[l, side, :KT])
            halo_x = khx[side] * (yh[l, side, KT] + hb[l, side, KT])
            unh[l, side, :KT] = halo
            unhx[l, side] = halo_x
            vs[:KT, at] = turn(vs[:KT, edge], halo)
            vs[KT, at] = turn(vs[KT, edge], halo_x)

        def body(t, carry):
            before, here, after = vs[:, t], vs[:, t + 1], vs[:, t + 2]
            q, p = explicit(r, before[:KT], here[:KT], after[:KT], here[KT], (after - before)[KT], ml[l, :, t], kl[:, t])
            qs[l, :, t] = q
            xs[l, :, t] = p
            extra = -r.a2 * (after[KT] + before[KT] - 2.0 * here[KT])
            px[l, t] = jnp.where(iota((SS, LN), 1) < 2, extra, 0.0)
            return carry

        lax.fori_loop(0, TT, body, 0)
    send_sums(local_solve(par, qs, xs, ss, w1, w3, k1, k3, et, lt, zo, phi, True), msg)


def last_kernel(par, got, pack, zl, ze, y2, kl, el, lt, out, tb, vb, os, sem):
    arrive(par, got, pack, tb, vb, None)
    copies = []
    for l in range(LEV):

        def rows(t, carry):
            own, _ = solved_rows(l, t, zl, ze, el, lt, tb, vb)
            own = kl[:, t] * (own + y2[l, :, t])
            for k in range(KT):
                os[l, k, pl.ds(t, SS, stride=TT), :] = own[k]
            return carry

        lax.fori_loop(0, TT, rows, 0)
        for k in range(KT):
            copies.append(pltpu.make_async_copy(os.at[l, k], out.at[l, :, pl.ds(k * LN, LN)], sem.at[l]))
            copies[-1].start()
    for c in copies:
        c.wait()


FIELD = (LEV, KT, TT, SS, LN)
EXTRA = (LEV, TT, SS, LN)
HALO = (LEV, 2, KT + 1, SS, LN)
FLUX = (LEV, 2, KT, SS, LN)


def call(kernel, outs, ins, scratch=(), out_specs=None, in_specs=None):
    return pl.pallas_call(
        kernel,
        out_shape=outs,
        in_specs=in_specs or [SM] + [VM] * (len(ins) - 1),
        out_specs=out_specs or [VM] * len(outs),
        scratch_shapes=list(scratch),
        compiler_params=PARAMS,
    )(*ins)


def vmem(*dims):
    return pltpu.VMEM(dims, F32)


def halo_rows(ensemble, mask):
    at = lax.axis_index("lat")
    first = jnp.concatenate([ensemble[:, 0, 0, :], mask[0:1, :]], axis=0).reshape(3, KT, LN)
    last = jnp.concatenate([ensemble[:, 0, ROWS - 1, :], mask[ROWS - 1 :, :]], axis=0).reshape(3, KT, LN)
    even = at % 2 == 0
    pairs = [(i, i + 1) for i in range(0, NLAT_DEV, 2)]
    odd_pairs = [(i, i + 1) for i in range(1, NLAT_DEV - 1, 2)]
    both = lambda edges: edges + [(j, i) for i, j in edges]
    one = lax.ppermute(jnp.where(even, last, first), "lat", both(pairs))
    two = lax.ppermute(jnp.where(even, first, last), "lat", both(odd_pairs))
    return jnp.where(even, two, one), jnp.where(even, one, two)


def parameters(level_rates):
    a = level_rates
    half = 0.5 / jnp.sqrt(a)
    theta = 2.0 * jnp.log1p(half + half * half / (1.0 + jnp.sqrt(1.0 + half * half)))
    scale = 1.0 / jnp.sqrt(1.0 + 4.0 * a)
    zero = jnp.zeros((LEV,), F32)
    table = jnp.stack([theta[0], theta[1], a[0], a[1], scale[0], scale[1], zero, zero], axis=1).reshape(-1)
    where = jnp.stack([lax.axis_index("lat"), lax.axis_index("lon")]).astype(F32)
    return jnp.concatenate([table, where])


def exchange(values, axis):
    return lax.all_to_all(values, axis, split_axis=0, concat_axis=0, tiled=True)


def shards(ensemble, cross_mix, sea_mask, level_rates, panel_inverse, reduced_lon, reduced_lat):
    par = parameters(level_rates)
    north, south = halo_rows(ensemble, sea_mask.astype(F32))
    work = [vmem(*FIELD), vmem(*FIELD), vmem(KT, TT, SS, LN)]
    carries = [vmem(LEV, KT + 1, SS, LN), vmem(LEV, KT + 1, SS, LN)]
    diffs = vmem(KT + 1, TT + 2, SS, LN)
    ul, ml, kl, w1, w3, k1, k3, et, lt, el = call(
        tables_kernel,
        [shape(*FIELD), shape(*FIELD), shape(KT, TT, SS, LN),
         shape(LEV, KT, LN, 2 * LN, dtype=BF16), shape(LEV, KT, LN, LN, dtype=BF16),
         shape(LEV, LN, 2 * LN, dtype=BF16), shape(LEV, LN, LN, dtype=BF16),
         shape(LEV, 2 * LN, COLS, dtype=BF16), shape(LEV, 8, TT, SS, LN), shape(LEV, 2, KT, SS, LN)],
        [par, ensemble[:, 0], cross_mix, sea_mask],
        [vmem(LEV, KT, ROWS, LN), vmem(LEV, KT, ROWS, LN), pltpu.VMEM((KT, ROWS, LN), jnp.int32),
         pltpu.SemaphoreType.DMA((5,))],
        in_specs=[SM, HB, HB, HB],
    )
    mats = [w1, w3, k1, k3, et, lt]
    solve_out = [shape(*FIELD), shape(*FLUX), shape(NLON_DEV, 8, LN)]
    carry_out = [shape(NLAT_DEV, PK, LN), shape(2, PK, LN), shape(*EXTRA)]
    zl, phi, msg, uh, kh = call(
        first_kernel,
        [shape(*FIELD), shape(*FLUX), shape(NLON_DEV, 24, LN), shape(*HALO), shape(2, KT + 1, SS, LN)],
        [par, ul, ml, kl, north, south] + mats,
        work,
    )
    got = exchange(msg, "lon")
    out, pack, ze, ux, kx, uhx, khx = call(
        functools.partial(carry_kernel, True),
        carry_out + [shape(*EXTRA), shape(TT, SS, LN), shape(LEV, 2, SS, LN), shape(2, SS, LN)],
        [par, got, phi, lt, el],
    )
    for step in range(2):
        got = exchange(out, "lat")
        y2, yx, yh, zl, phi, msg, px = call(
            half_kernel,
            [shape(*FIELD), shape(*EXTRA), shape(*HALO)] + solve_out + [shape(*EXTRA)],
            [par, got, pack, zl, ze, ul, ux, uh, uhx, ml, el] + mats,
            carries + [diffs] + work,
        )
        got = exchange(msg, "lon")
        out, pack, ze = call(functools.partial(carry_kernel, False), carry_out, [par, got, phi, px, lt, el])
        got = exchange(out, "lat")
        if step == 1:
            break
        ul, ux, uh, uhx, zl, phi, msg, px = call(
            step_kernel,
            [shape(*FIELD), shape(*EXTRA), shape(*HALO), shape(LEV, 2, SS, LN)] + solve_out + [shape(*EXTRA)],
            [par, got, pack, zl, ze, y2, yx, yh, kl, kx, kh, khx, ml, el] + mats,
            carries + [vmem(*HALO), diffs] + work,
        )
        got = exchange(msg, "lon")
        out, pack, ze = call(functools.partial(carry_kernel, False), carry_out, [par, got, phi, px, lt, el])
    (final,) = call(
        last_kernel,
        [shape(LEV, ROWS, COLS)],
        [par, got, pack, zl, ze, y2, kl, el, lt],
        carries + [vmem(LEV, KT, ROWS, LN), pltpu.SemaphoreType.DMA((LEV,))],
        out_specs=[HB],
    )
    return final[:, None]


def solution(mesh):
    in_specs = (
        P(None, None, "lat", "lon"),
        P(None, "lat", "lon"),
        P("lat", "lon"),
        P(),
        P(),
        P(),
        P(),
    )
    out_specs = P(None, None, "lat", "lon")
    return jax.shard_map(shards, mesh=mesh, in_specs=in_specs, out_specs=out_specs, check_vma=False)
```

```python
import functools

import jax
import jax.numpy as jnp
from jax import lax
from jax.experimental import pallas as pl
from jax.experimental.pallas import tpu as pltpu
from jax.sharding import PartitionSpec as P

LEV, ROWS, COLS = 2, 128, 2048
KT, TT, SS, LN = 16, 16, 8, 128
NLAT_DEV, NLON_DEV = 16, 8
NLAT, NLON = ROWS * NLAT_DEV, COLS * NLON_DEV
F32, BF16 = jnp.float32, jnp.bfloat16
VM = pl.BlockSpec(memory_space=pltpu.VMEM)
SM = pl.BlockSpec(memory_space=pltpu.SMEM)
HB = pl.BlockSpec(memory_space=pltpu.HBM)
PARAMS = pltpu.CompilerParams(vmem_limit_bytes=10 * 1024 * 1024)

L_P, L_LQ, L_Q, L_CQ, L_CQL, L_CP, L_GQ, L_GP = range(8)
PK = 40


def shape(*dims, dtype=F32):
    return jax.ShapeDtypeStruct(dims, dtype)


def iota(dims, axis):
    return lax.broadcasted_iota(jnp.int32, dims, axis)


def fiota(dims, axis):
    return iota(dims, axis).astype(F32)


class Rates:
    def __init__(self, par, level):
        self.t1, self.t2, self.a1, self.a2, self.c1, self.c2 = (par[2 * i + level] for i in range(6))


def position(par):
    return par[12], par[13]


def split3(x):
    high = x.astype(BF16)
    rest = x - high.astype(F32)
    mid = rest.astype(BF16)
    return high, mid, (rest - mid.astype(F32)).astype(BF16)


def dot(x, y):
    return jnp.dot(x, y, preferred_element_type=F32)


def tables_kernel(par, u_hbm, m_hbm, k_hbm, ul, ml, kl, w1, w3, k1, k3, et, lt, el, su, sm, sk, sem):
    copies = []
    for l in range(LEV):
        copies.append([pltpu.make_async_copy(u_hbm.at[l, :, pl.ds(k * LN, LN)], su.at[l, k], sem.at[l]) for k in range(KT)])
    for l in range(LEV):
        copies.append([pltpu.make_async_copy(m_hbm.at[l, :, pl.ds(k * LN, LN)], sm.at[l, k], sem.at[2 + l]) for k in range(KT)])
    copies.append([pltpu.make_async_copy(k_hbm.at[:, pl.ds(k * LN, LN)], sk.at[k], sem.at[4]) for k in range(KT)])
    for group in copies:
        for c in group:
            c.start()
    i_pos, _ = position(par)
    for l in range(LEV):
        r = Rates(par, l)
        dist = jnp.abs(fiota((LN, LN), 0) - fiota((LN, LN), 1))
        high, mid, low = split3(r.c1 * jnp.exp(-r.t1 * dist))
        k1[l] = jnp.concatenate([high, mid], axis=1)
        k3[l] = low
        lane = iota((LN, LN), 1)
        row = fiota((LN, LN), 0)
        slot = lane % 32
        rising = ((lane < 96) & (slot >= 16)) | (lane == 97)
        base = jnp.exp(-r.t1 * jnp.where(rising, row, (LN - 1) - row))

        def weights(k, carry):
            kf = k.astype(F32)
            pick = jnp.where((lane < 96) & (slot % 16 == k), 1.0, 0.0)
            pick = jnp.where(lane == 96, jnp.exp(-r.t1 * (LN * (KT - 1 - kf))), pick)
            pick = jnp.where(lane == 97, jnp.exp(-r.t1 * (LN * kf)), pick)
            high, mid, low = split3(base * pick)
            w1[l, k] = jnp.concatenate([high, mid], axis=1)
            w3[l, k] = low
            return carry

        lax.fori_loop(0, KT, weights, 0)
        slot = iota((32, LN), 0)
        col = fiota((32, LN), 1)
        own = (slot % 16).astype(F32)
        for k in range(KT):
            gap = jnp.where(slot < 16, k - own, own - k)
            power = (gap - 1) * LN + jnp.where(slot < 16, col + 1, LN - col)
            value = jnp.where(gap > 0, r.c1 * jnp.exp(-r.t1 * jnp.maximum(power, 0.0)), 0.0)
            high, mid, low = split3(value)
            zero = jnp.zeros_like(high)
            et[l, :, pl.ds(k * LN, LN)] = jnp.concatenate([high, mid, low, zero, high, mid, high, zero], axis=0)
        lane_f = fiota((SS, LN), 1)
        for k in range(KT):
            el[l, 0, k] = r.c1 * jnp.exp(-r.t1 * (k * LN + lane_f + 1.0))
            el[l, 1, k] = r.c1 * jnp.exp(-r.t1 * (COLS - k * LN - lane_f))
        sub = fiota((SS, LN), 0)
        scale = r.c2 / (1.0 - jnp.exp(jnp.full((SS, LN), -2.0 * (NLAT + 1), F32) * r.t2))
        for t in range(TT):
            local = sub * TT + t
            index = local + i_pos * ROWS
            p = 1.0 - jnp.exp(-2.0 * r.t2 * (index + 1.0))
            q = 1.0 - jnp.exp(-2.0 * r.t2 * (NLAT - index))
            lt[l, L_P, t] = p
            lt[l, L_Q, t] = q
            lt[l, L_LQ, t] = q * jnp.exp(jnp.full((SS, LN), -float(t), F32) * r.t2)
            lt[l, L_CQ, t] = scale * q
            lt[l, L_CQL, t] = scale * q * jnp.exp(jnp.full((SS, LN), -float(t + 1), F32) * r.t2)
            lt[l, L_CP, t] = scale * p
            lt[l, L_GQ, t] = scale * q * jnp.exp(-r.t2 * (local + 1.0))
            lt[l, L_GP, t] = scale * p * jnp.exp(-r.t2 * (ROWS - local))
    for group in copies:
        for c in group:
            c.wait()

    def move(k, carry):
        for t in range(TT):
            for l in range(LEV):
                ul[l, k, t] = su[l, k, pl.ds(t, SS, stride=TT), :]
                ml[l, k, t] = sm[l, k, pl.ds(t, SS, stride=TT), :]
            kl[k, t] = sk[k, pl.ds(t, SS, stride=TT), :].astype(F32)
        return carry

    lax.fori_loop(0, KT, move, 0)


def turned(tiles, ext):
    lane = iota((SS, LN), 1)
    at_end, at_start = lane == LN - 1, lane == 0
    zero = jnp.zeros((SS, LN), F32)
    before = zero if ext is None else ext
    right = pltpu.roll(tiles(0), LN - 1, 1)
    for k in range(KT):
        if k + 1 < KT:
            beyond = pltpu.roll(tiles(k + 1), LN - 1, 1)
        else:
            beyond = zero if ext is None else pltpu.roll(ext, LN - 2, 1)
        left = pltpu.roll(tiles(k), 1, 1)
        yield jnp.where(at_end, beyond, right), jnp.where(at_start, before, left)
        right, before = beyond, left


def north_of(last, halo):
    return jnp.where(iota(last.shape, last.ndim - 2) == 0, halo, pltpu.roll(last, 1, last.ndim - 2))


def south_of(first, halo):
    return jnp.where(iota(first.shape, first.ndim - 2) == SS - 1, halo, pltpu.roll(first, SS - 1, first.ndim - 2))


def down_scan(x, t2):
    sub = iota(x.shape, x.ndim - 2)
    x = jnp.where(sub >= 1, pltpu.roll(x, 1, x.ndim - 2), 0.0)
    for step in (1, 2, 4):
        factor = jnp.exp(jnp.full((SS, LN), -float(TT * step), F32) * t2)
        x = x + factor * jnp.where(sub >= step, pltpu.roll(x, step, x.ndim - 2), 0.0)
    return x


def up_scan(x, t2):
    sub = iota(x.shape, x.ndim - 2)
    x = jnp.where(sub < SS - 1, pltpu.roll(x, SS - 1, x.ndim - 2), 0.0)
    for step in (1, 2, 4):
        factor = jnp.exp(jnp.full((SS, LN), -float(TT * step), F32) * t2)
        x = x + factor * jnp.where(sub < SS - step, pltpu.roll(x, SS - step, x.ndim - 2), 0.0)
    return x


def chunk_ends(last, acc, t2):
    carry_down = down_scan(last, t2)
    carry_up = up_scan(acc, t2)
    step = jnp.exp(jnp.full((SS, LN), -float(TT), F32) * t2)
    phi = (last + step * carry_down)[..., SS - 1 : SS, :]
    psi = (acc + step * carry_up)[..., 0:1, :]
    return carry_down, carry_up, jnp.broadcast_to(phi, last.shape), jnp.broadcast_to(psi, last.shape)


def lam2(t2):
    return jnp.exp(jnp.full((SS, LN), -1.0, F32) * t2)


def local_solve(par, qs, xs, ss, w1, w3, k1, k3, et, lt, zl, phi, with_p):
    sums = []
    for l in range(LEV):
        r = Rates(par, l)

        def tile(k, ab):
            high, mid, low = split3(qs[l, k].reshape(ROWS, LN))
            lhs1 = jnp.concatenate([high, mid], axis=1)
            lhs2 = jnp.concatenate([low, high], axis=1)
            kk = k1[l]
            one = dot(lhs1, jnp.concatenate([kk, kk], axis=0))
            two = dot(lhs2, jnp.concatenate([kk[:, :LN], k3[l]], axis=0))
            x = (one[:, :LN] + one[:, LN:] + two).reshape(TT, SS, LN)
            xs[l, k] = xs[l, k] + x if with_p else x
            ww = w1[l, k]
            one = dot(lhs1, jnp.concatenate([ww, ww], axis=0))
            two = dot(lhs2, jnp.concatenate([ww[:, :LN], w3[l, k]], axis=0))
            return ab + (one[:, :LN] + one[:, LN:] + two)

        ab = jnp.zeros((ROWS, LN), F32)
        for k in range(KT):
            ab = tile(k, ab)
        sums.append(ab)
        high, mid, low = split3(ab)
        lane = iota((ROWS, LN), 1)
        second = jnp.where(lane < 64, mid.astype(F32), low.astype(F32)).astype(BF16)
        lhs = jnp.concatenate([high, second], axis=1)
        for k in range(0, KT, 2):
            fix = dot(lhs, et[l, :, pl.ds(k * LN, 2 * LN)])
            xs[l, k] += fix[:, :LN].reshape(TT, SS, LN)
            xs[l, k + 1] += fix[:, LN:].reshape(TT, SS, LN)

        lam = lam2(r.t2)

        def down(t, carry):
            s, acc = carry
            x = xs[l, :, t]
            s = lam * s + lt[l, L_P, t] * x
            ss[:, t] = s
            return s, acc + lt[l, L_LQ, t] * x

        zero = jnp.zeros((KT, SS, LN), F32)
        last, acc = zero, zero
        for t in range(TT):
            last, acc = down(t, (last, acc))
        carry_down, carry_up, phi_l, psi_l = chunk_ends(last, acc, r.t2)
        phi[l, 0] = phi_l
        phi[l, 1] = psi_l

        def up(i, u):
            t = TT - 1 - i
            zl[l, :, t] = lt[l, L_CQ, t] * ss[:, t] + lt[l, L_CQL, t] * carry_down + lt[l, L_CP, t] * u
            return lam * (u + lt[l, L_Q, t] * xs[l, :, t])

        u = lam * carry_up
        for i in range(TT):
            u = up(i, u)
    return sums


def explicit(r, l, t, before, here, after, ext_here, ext_diff, ml, kl, qs, xs):
    here = [here(k) for k in range(KT)]
    around = []
    diff = []
    for k in range(KT):
        up, down = before(k), after(k)
        around.append(down + up - 2.0 * here[k])
        diff.append(down - up)
    flat = zip(turned(lambda k: here[k], ext_here), turned(lambda k: diff[k], ext_diff))
    for k, ((east, west), (diff_east, diff_west)) in enumerate(flat):
        lon = east + west - 2.0 * here[k]
        inner = here[k] + ml[l, k, t] * (diff_east - diff_west) + (2.0 * r.a1) * lon + (2.0 * r.a2) * around[k]
        qs[l, k, t] = kl[k, t] * inner - r.a1 * lon
        xs[l, k, t] = -r.a2 * around[k]


def end_columns(first, last):
    lane = iota((ROWS, LN), 1)
    turned = jnp.where(lane < 64, first, last).T
    return turned[0:1], turned[LN - 1 : LN]


def first_kernel(par, ul, ml, kl, north, south, w1, w3, k1, k3, et, lt, zl, phi, msg, uh, kh, qs, xs, ss):
    def spread(ref, row):
        return jnp.stack([jnp.broadcast_to(ref[row, k : k + 1, :], (SS, LN)) for k in range(KT)])

    for side, ref in ((0, north), (1, south)):
        kh[side, :KT] = spread(ref, 2)
    for l in range(LEV):
        r = Rates(par, l)
        uh[l, 0, :KT] = spread(north, l)
        uh[l, 1, :KT] = spread(south, l)

        for t in range(TT):
            if t == 0:
                before = lambda k: north_of(ul[l, k, TT - 1], uh[l, 0, k])
            else:
                before = lambda k, t=t: ul[l, k, t - 1]
            if t == TT - 1:
                after = lambda k: south_of(ul[l, k, 0], uh[l, 1, k])
            else:
                after = lambda k, t=t: ul[l, k, t + 1]
            explicit(r, l, t, before, lambda k, t=t: ul[l, k, t], after, None, None, ml, kl, qs, xs)
    sums = local_solve(par, qs, xs, ss, w1, w3, k1, k3, et, lt, zl, phi, True)
    parts = []
    for l in range(LEV):
        parts.append(sums[l].T[96:98])
    for l in range(LEV):
        parts.extend(end_columns(ul[l, 0].reshape(ROWS, LN), ul[l, KT - 1].reshape(ROWS, LN)))
    for l in range(LEV):
        parts.extend(end_columns(ml[l, 0].reshape(ROWS, LN), ml[l, KT - 1].reshape(ROWS, LN)))
    parts.extend(end_columns(kl[0].reshape(ROWS, LN), kl[KT - 1].reshape(ROWS, LN)))
    lane = iota((1, LN), 1)
    for row in range(3):
        n0, s0 = north[row, 0:1, :], south[row, 0:1, :]
        n1, s1 = north[row, KT - 1 : KT, :], south[row, KT - 1 : KT, :]
        parts.append(jnp.where(lane == 0, n0, pltpu.roll(s0, 1, 1)))
        parts.append(jnp.where(lane == LN - 1, n1, pltpu.roll(s1, LN - 1, 1)))
    parts.append(jnp.zeros((4, LN), F32))
    block = jnp.concatenate(parts, axis=0)
    for j in range(NLON_DEV):
        msg[j] = block


def row_after(x, halo):
    lane = iota(x.shape, 1)
    y = jnp.where(lane >= LN - SS, pltpu.roll(x, LN - SS - 1, 1), pltpu.roll(x, LN - SS, 1))
    return jnp.where(lane == LN - 1, halo, y)


def row_before(x, halo):
    lane = iota(x.shape, 1)
    y = jnp.where(lane < SS, pltpu.roll(x, SS + 1, 1), pltpu.roll(x, SS, 1))
    return jnp.where(lane == 0, halo, y)


def lane_value(x, index):
    return jnp.sum(jnp.where(iota(x.shape, x.ndim - 1) == index, x, 0.0), axis=-1, keepdims=True)


def as_tile(rows):
    count = sum(r.shape[0] for r in rows)
    return jnp.concatenate(rows + [jnp.zeros((LN - count, LN), F32)], axis=0).T.reshape(TT, SS, LN)


def carry_kernel(first, *refs):
    if first:
        par, got, phi, lt, el, out, pack, ze, ux, kx, uhx, khx = refs
    else:
        par, got, phi, px, lt, el, out, pack, ze = refs
    i_pos, j_pos = position(par)
    peer = fiota((NLON_DEV, LN), 0)
    mine = peer == j_pos
    fluxes = []
    ext = []
    if first:
        kw = pltpu.roll(got[:, 13, :], 1, 0)
        ke = pltpu.roll(got[:, 12, :], NLON_DEV - 1, 0)
        kw_end = pltpu.roll(got[:, 19, :], 1, 0)
        ke_end = pltpu.roll(got[:, 18, :], NLON_DEV - 1, 0)

        def own(x):
            return jnp.sum(jnp.where(mine, x, 0.0), axis=0, keepdims=True)

        def corners(west_end, east_end):
            lane = iota((1, LN), 1)
            w, e = own(west_end), own(east_end)
            w_n, w_s = lane_value(w, LN - 1), lane_value(w, LN - 2)
            e_n, e_s = lane_value(e, 0), lane_value(e, 1)
            pick = lambda a, b: jnp.broadcast_to(jnp.where(lane == 0, a, jnp.where(lane == 1, b, 0.0)), (SS, LN))
            return pick(w_n, e_n), pick(w_s, e_s)

        khx[0], khx[1] = corners(kw_end, ke_end)
        kx[...] = as_tile([own(kw), own(ke)])
    for l in range(LEV):
        r = Rates(par, l)
        a, b = got[:, 2 * l, :], got[:, 2 * l + 1, :]
        one = jnp.full((NLON_DEV, LN), 1.0, F32)
        if first:
            uw = pltpu.roll(got[:, 5 + 2 * l, :], 1, 0)
            ue = pltpu.roll(got[:, 4 + 2 * l, :], NLON_DEV - 1, 0)
            uw_end = pltpu.roll(got[:, 15 + 2 * l, :], 1, 0)
            ue_end = pltpu.roll(got[:, 14 + 2 * l, :], NLON_DEV - 1, 0)
            w_up = row_before(uw, jnp.sum(jnp.where(iota(uw.shape, 1) == LN - 1, uw_end, 0.0), axis=1, keepdims=True))
            w_dn = row_after(uw, jnp.sum(jnp.where(iota(uw.shape, 1) == LN - 2, uw_end, 0.0), axis=1, keepdims=True))
            e_up = row_before(ue, jnp.sum(jnp.where(iota(ue.shape, 1) == 0, ue_end, 0.0), axis=1, keepdims=True))
            e_dn = row_after(ue, jnp.sum(jnp.where(iota(ue.shape, 1) == 1, ue_end, 0.0), axis=1, keepdims=True))
            m0, mn, k0, kn = got[:, 8 + 2 * l, :], got[:, 9 + 2 * l, :], got[:, 12, :], got[:, 13, :]
            h0 = k0 * (m0 * (w_up - w_dn) + 2.0 * r.a1 * uw) - r.a1 * uw
            hn = kn * (mn * (e_dn - e_up) + 2.0 * r.a1 * ue) - r.a1 * ue
            far = jnp.exp(-(COLS - 1.0) * r.t1 * one)
            a = a + far * h0 + hn
            b = b + h0 + far * hn
        whole = 1.0 - jnp.exp(-float(NLON) * r.t1 * one)
        back = j_pos - peer - 1.0
        back = jnp.where(back < 0, back + NLON_DEV, back)
        ahead = peer - j_pos - 1.0
        ahead = jnp.where(ahead < 0, ahead + NLON_DEV, ahead)
        left = jnp.sum(a * (jnp.exp(-r.t1 * COLS * back) / whole), axis=0, keepdims=True)
        right = jnp.sum(b * (jnp.exp(-r.t1 * COLS * ahead) / whole), axis=0, keepdims=True)
        a = jnp.sum(jnp.where(mine, a, 0.0), axis=0, keepdims=True)
        b = jnp.sum(jnp.where(mine, b, 0.0), axis=0, keepdims=True)
        lam = jnp.exp(-r.t1 * jnp.full((1, LN), 1.0, F32))
        far = jnp.exp(-(COLS + 1.0) * r.t1 * jnp.full((1, LN), 1.0, F32))
        xw = r.c1 * (left + lam * b + far * right)
        xe = r.c1 * (right + lam * a + far * left)
        if first:
            pw = -r.a2 * (w_dn + w_up - 2.0 * uw)
            pe = -r.a2 * (e_dn + e_up - 2.0 * ue)
            xw = xw + own(pw)
            xe = xe + own(pe)
            left = left + own(h0) / lam
            right = right + own(hn) / lam
            ux[l] = as_tile([own(uw), own(ue)])
            uhx[l, 0], uhx[l, 1] = corners(uw_end, ue_end)
        x = as_tile([xw, xe, left, right])
        if not first:
            x = x + px[l]
        ext.append(x)
    lams = [lam2(Rates(par, l).t2) for l in range(LEV)]
    zero = jnp.zeros((SS, LN), F32)
    state = [zero, zero]
    acc = [zero, zero]
    kept = [[], []]
    for t in range(TT):
        for l in range(LEV):
            state[l] = lams[l] * state[l] + lt[l, L_P, t] * ext[l][t]
            acc[l] = acc[l] + lt[l, L_LQ, t] * ext[l][t]
            kept[l].append(state[l])
    for l in range(LEV):
        r = Rates(par, l)
        carry_down, carry_up, phi_e, psi_e = chunk_ends(state[l], acc[l], r.t2)
        u = lams[l] * carry_up
        for t in range(TT - 1, -1, -1):
            ze[l, t] = lt[l, L_CQ, t] * kept[l][t] + lt[l, L_CQL, t] * carry_down + lt[l, L_CP, t] * u
            u = lams[l] * (u + lt[l, L_Q, t] * ext[l][t])
        pair = []
        for side, flux in ((0, phi_e), (1, psi_e)):
            tiles = phi[l, side] + lane_value(flux, 2) * el[l, 0] + lane_value(flux, 3) * el[l, 1]
            pair.append([tiles[k] for k in range(KT)] + [flux])
        fluxes.append(pair)
    sub = iota((SS, LN), 0)
    packed = []
    for side in (0, 1):
        rows = fluxes[0][side] + fluxes[1][side]
        rows = rows + [zero] * (PK - len(rows))
        vregs = []
        for v in range(PK // SS):
            y = rows[v * SS]
            for j in range(1, SS):
                y = jnp.where(sub == j, rows[v * SS + j], y)
            vregs.append(y)
        packed.append(jnp.concatenate(vregs, axis=0))
        pack[side] = packed[side]
    t2 = level_rows(Rates(par, 0).t2, Rates(par, 1).t2)
    for p in range(NLAT_DEV):
        away = jnp.maximum(jnp.abs(p - i_pos) - 1.0, 0.0)
        factor = jnp.exp(-(ROWS * away) * t2)
        ahead = jnp.full((PK, LN), p - i_pos, F32) > 0
        out[p] = factor * jnp.where(ahead, packed[0], packed[1])


def level_rows(low, high):
    return jnp.where(iota((PK, LN), 0) <= KT, low, high)


def arrive(par, got, pack, tb, vb, hb):
    i_pos, _ = position(par)
    zero = jnp.zeros((PK, LN), F32)
    above, below = zero, zero
    for p in range(NLAT_DEV):
        side = jnp.full((PK, LN), p - i_pos, F32)
        above = above + jnp.where(side < 0, got[p], 0.0)
        below = below + jnp.where(side > 0, got[p], 0.0)
    t2 = level_rows(Rates(par, 0).t2, Rates(par, 1).t2)
    scale = level_rows(Rates(par, 0).c2, Rates(par, 1).c2) / (1.0 - jnp.exp(-2.0 * (NLAT + 1) * t2))
    lam = jnp.exp(-t2)
    block = jnp.exp(-float(ROWS) * t2)
    start = i_pos * ROWS
    q_n = 1.0 - jnp.exp(-2.0 * t2 * (NLAT + 1.0 - start))
    p_n = 1.0 - jnp.exp(-2.0 * t2 * start)
    q_s = 1.0 - jnp.exp(-2.0 * t2 * (NLAT - ROWS - start))
    p_s = 1.0 - jnp.exp(-2.0 * t2 * (ROWS + 1.0 + start))
    north = scale * (q_n * above + p_n * lam * (pack[1] + block * below))
    south = scale * (q_s * lam * (pack[0] + block * above) + p_s * below)
    for l in range(LEV):
        for k in range(KT + 1):
            at = l * (KT + 1) + k
            wide = lambda x: jnp.broadcast_to(x[at : at + 1], (SS, LN))
            tb[l, k] = wide(above)
            vb[l, k] = wide(below)
            if hb is not None:
                hb[l, 0, k] = wide(north)
                hb[l, 1, k] = wide(south)


def solved_rows(l, zl, ze, el, lt, tb, vb, use, use_extra):
    step = 4
    for start in range(0, TT, step):
        times = range(start, start + step)
        extra = [ze[l, t] for t in times]
        gq = [lt[l, L_GQ, t] for t in times]
        gp = [lt[l, L_GP, t] for t in times]
        z_left = [jnp.broadcast_to(x[:, 2:3], (SS, LN)) for x in extra]
        z_right = [jnp.broadcast_to(x[:, 3:4], (SS, LN)) for x in extra]
        for k in range(KT):
            e_left, e_right, above, below = el[l, 0, k], el[l, 1, k], tb[l, k], vb[l, k]
            for i, t in enumerate(times):
                use(k, t, zl[l, k, t] + e_left * z_left[i] + e_right * z_right[i] + gq[i] * above + gp[i] * below)
        if use_extra is not None:
            above, below = tb[l, KT], vb[l, KT]
            for i, t in enumerate(times):
                use_extra(t, extra[i] + gq[i] * above + gp[i] * below)


def send_sums(sums, msg):
    block = jnp.concatenate([s.T[96:98] for s in sums] + [jnp.zeros((4, LN), F32)], axis=0)
    for j in range(NLON_DEV):
        msg[j] = block


def half_kernel(par, got, pack, zl, ze, ul, ux, uh, uhx, ml, el, w1, w3, k1, k3, et, lt,
                y2, yx, yh, zo, phi, msg, px, tb, vb, vs, qs, xs, ss):
    arrive(par, got, pack, tb, vb, yh)
    for l in range(LEV):
        r = Rates(par, l)

        def use(k, t, own):
            y2[l, k, t] = own
            vs[k, t + 1] = own - ul[l, k, t]

        def use_extra(t, extra):
            yx[l, t] = extra
            vs[KT, t + 1] = extra - ux[l, t]
            px[l, t] = jnp.zeros((SS, LN), F32)

        solved_rows(l, zl, ze, el, lt, tb, vb, use, use_extra)
        for side, edge, at, turn in ((0, TT, 0, north_of), (1, 1, TT + 1, south_of)):
            vs[:KT, at] = turn(vs[:KT, edge], yh[l, side, :KT] - uh[l, side, :KT])
            vs[KT, at] = turn(vs[KT, edge], yh[l, side, KT] - uhx[l, side])

        for t in range(TT):
            diff = [vs[k, t + 2] - vs[k, t] for k in range(KT + 1)]
            for k, (east, west) in enumerate(turned(lambda k: diff[k], diff[KT])):
                qs[l, k, t] = 0.5 * ml[l, k, t] * (east - west)
    send_sums(local_solve(par, qs, xs, ss, w1, w3, k1, k3, et, lt, zo, phi, False), msg)


def step_kernel(par, got, pack, zl, ze, y2, yx, yh, kl, kx, kh, khx, ml, el, w1, w3, k1, k3, et, lt,
                un, unx, unh, unhx, zo, phi, msg, px, tb, vb, hb, vs, qs, xs, ss):
    arrive(par, got, pack, tb, vb, hb)
    for l in range(LEV):
        r = Rates(par, l)

        def use(k, t, own):
            own = kl[k, t] * (own + y2[l, k, t])
            un[l, k, t] = own
            vs[k, t + 1] = own

        def use_extra(t, extra):
            extra = kx[t] * (extra + yx[l, t])
            unx[l, t] = extra
            vs[KT, t + 1] = extra

        solved_rows(l, zl, ze, el, lt, tb, vb, use, use_extra)
        for side, edge, at, turn in ((0, TT, 0, north_of), (1, 1, TT + 1, south_of)):
            halo = kh[side, :KT] * (yh[l, side, :KT] + hb[l, side, :KT])
            halo_x = khx[side] * (yh[l, side, KT] + hb[l, side, KT])
            unh[l, side, :KT] = halo
            unhx[l, side] = halo_x
            vs[:KT, at] = turn(vs[:KT, edge], halo)
            vs[KT, at] = turn(vs[KT, edge], halo_x)

        for t in range(TT):
            before, here, after = vs[KT, t], vs[KT, t + 1], vs[KT, t + 2]
            explicit(r, l, t, lambda k: vs[k, t], lambda k: vs[k, t + 1], lambda k: vs[k, t + 2],
                     here, after - before, ml, kl, qs, xs)
            px[l, t] = jnp.where(iota((SS, LN), 1) < 2, -r.a2 * (after + before - 2.0 * here), 0.0)
    send_sums(local_solve(par, qs, xs, ss, w1, w3, k1, k3, et, lt, zo, phi, True), msg)


def last_kernel(par, got, pack, zl, ze, y2, kl, el, lt, out, tb, vb, os, sem):
    arrive(par, got, pack, tb, vb, None)
    copies = []
    for l in range(LEV):

        def use(k, t, own):
            os[l, k, pl.ds(t, SS, stride=TT), :] = kl[k, t] * (own + y2[l, k, t])

        solved_rows(l, zl, ze, el, lt, tb, vb, use, None)
        for k in range(KT):
            copies.append(pltpu.make_async_copy(os.at[l, k], out.at[l, :, pl.ds(k * LN, LN)], sem.at[l]))
            copies[-1].start()
    for c in copies:
        c.wait()


FIELD = (LEV, KT, TT, SS, LN)
EXTRA = (LEV, TT, SS, LN)
HALO = (LEV, 2, KT + 1, SS, LN)
FLUX = (LEV, 2, KT, SS, LN)


def call(kernel, outs, ins, scratch=(), out_specs=None, in_specs=None):
    return pl.pallas_call(
        kernel,
        out_shape=outs,
        in_specs=in_specs or [SM] + [VM] * (len(ins) - 1),
        out_specs=out_specs or [VM] * len(outs),
        scratch_shapes=list(scratch),
        compiler_params=PARAMS,
    )(*ins)


def vmem(*dims):
    return pltpu.VMEM(dims, F32)


def halo_rows(ensemble, mask):
    at = lax.axis_index("lat")
    first = jnp.concatenate([ensemble[:, 0, 0, :], mask[0:1, :].astype(F32)], axis=0).reshape(3, KT, LN)
    last = jnp.concatenate([ensemble[:, 0, ROWS - 1, :], mask[ROWS - 1 :, :].astype(F32)], axis=0).reshape(3, KT, LN)
    even = at % 2 == 0
    pairs = [(i, i + 1) for i in range(0, NLAT_DEV, 2)]
    odd_pairs = [(i, i + 1) for i in range(1, NLAT_DEV - 1, 2)]
    both = lambda edges: edges + [(j, i) for i, j in edges]
    one = lax.ppermute(jnp.where(even, last, first), "lat", both(pairs))
    two = lax.ppermute(jnp.where(even, first, last), "lat", both(odd_pairs))
    return jnp.where(even, two, one), jnp.where(even, one, two)


def parameters(level_rates):
    a = level_rates
    half = 0.5 / jnp.sqrt(a)
    theta = 2.0 * jnp.log1p(half + half * half / (1.0 + jnp.sqrt(1.0 + half * half)))
    scale = 1.0 / jnp.sqrt(1.0 + 4.0 * a)
    where = jnp.stack([lax.axis_index("lat"), lax.axis_index("lon")]).astype(F32)
    return jnp.concatenate([jnp.stack([theta, a, scale]).reshape(-1), where])


def exchange(values, axis):
    return lax.all_to_all(values, axis, split_axis=0, concat_axis=0, tiled=True)


def shards(ensemble, cross_mix, sea_mask, level_rates, panel_inverse, reduced_lon, reduced_lat):
    par = parameters(level_rates)
    north, south = halo_rows(ensemble, sea_mask)
    work = [vmem(*FIELD), vmem(*FIELD), vmem(KT, TT, SS, LN)]
    carries = [vmem(LEV, KT + 1, SS, LN), vmem(LEV, KT + 1, SS, LN)]
    diffs = vmem(KT + 1, TT + 2, SS, LN)
    ul, ml, kl, w1, w3, k1, k3, et, lt, el = call(
        tables_kernel,
        [shape(*FIELD), shape(*FIELD), shape(KT, TT, SS, LN),
         shape(LEV, KT, LN, 2 * LN, dtype=BF16), shape(LEV, KT, LN, LN, dtype=BF16),
         shape(LEV, LN, 2 * LN, dtype=BF16), shape(LEV, LN, LN, dtype=BF16),
         shape(LEV, 2 * LN, COLS, dtype=BF16), shape(LEV, 8, TT, SS, LN), shape(LEV, 2, KT, SS, LN)],
        [par, ensemble[:, 0], cross_mix, sea_mask],
        [vmem(LEV, KT, ROWS, LN), vmem(LEV, KT, ROWS, LN), pltpu.VMEM((KT, ROWS, LN), jnp.int32),
         pltpu.SemaphoreType.DMA((5,))],
        in_specs=[SM, HB, HB, HB],
    )
    mats = [w1, w3, k1, k3, et, lt]
    solve_out = [shape(*FIELD), shape(*FLUX), shape(NLON_DEV, 8, LN)]
    carry_out = [shape(NLAT_DEV, PK, LN), shape(2, PK, LN), shape(*EXTRA)]
    zl, phi, msg, uh, kh = call(
        first_kernel,
        [shape(*FIELD), shape(*FLUX), shape(NLON_DEV, 24, LN), shape(*HALO), shape(2, KT + 1, SS, LN)],
        [par, ul, ml, kl, north, south] + mats,
        work,
    )
    got = exchange(msg, "lon")
    out, pack, ze, ux, kx, uhx, khx = call(
        functools.partial(carry_kernel, True),
        carry_out + [shape(*EXTRA), shape(TT, SS, LN), shape(LEV, 2, SS, LN), shape(2, SS, LN)],
        [par, got, phi, lt, el],
    )
    for step in range(2):
        got = exchange(out, "lat")
        y2, yx, yh, zl, phi, msg, px = call(
            half_kernel,
            [shape(*FIELD), shape(*EXTRA), shape(*HALO)] + solve_out + [shape(*EXTRA)],
            [par, got, pack, zl, ze, ul, ux, uh, uhx, ml, el] + mats,
            carries + [diffs] + work,
        )
        got = exchange(msg, "lon")
        out, pack, ze = call(functools.partial(carry_kernel, False), carry_out, [par, got, phi, px, lt, el])
        got = exchange(out, "lat")
        if step == 1:
            break
        ul, ux, uh, uhx, zl, phi, msg, px = call(
            step_kernel,
            [shape(*FIELD), shape(*EXTRA), shape(*HALO), shape(LEV, 2, SS, LN)] + solve_out + [shape(*EXTRA)],
            [par, got, pack, zl, ze, y2, yx, yh, kl, kx, kh, khx, ml, el] + mats,
            carries + [vmem(*HALO), diffs] + work,
        )
        got = exchange(msg, "lon")
        out, pack, ze = call(functools.partial(carry_kernel, False), carry_out, [par, got, phi, px, lt, el])
    (final,) = call(
        last_kernel,
        [shape(LEV, ROWS, COLS)],
        [par, got, pack, zl, ze, y2, kl, el, lt],
        carries + [vmem(LEV, KT, ROWS, LN), pltpu.SemaphoreType.DMA((LEV,))],
        out_specs=[HB],
    )
    return final[:, None]


def solution(mesh):
    in_specs = (
        P(None, None, "lat", "lon"),
        P(None, "lat", "lon"),
        P("lat", "lon"),
        P(),
        P(),
        P(),
        P(),
    )
    out_specs = P(None, None, "lat", "lon")
    return jax.shard_map(shards, mesh=mesh, in_specs=in_specs, out_specs=out_specs, check_vma=False)
```

```python
import functools

import jax
import jax.numpy as jnp
from jax import lax
from jax.experimental import pallas as pl
from jax.experimental.pallas import tpu as pltpu
from jax.sharding import PartitionSpec as P

LEV, ROWS, COLS = 2, 128, 2048
KT, TT, SS, LN = 16, 16, 8, 128
NLAT_DEV, NLON_DEV = 16, 8
NLAT, NLON = ROWS * NLAT_DEV, COLS * NLON_DEV
F32, BF16 = jnp.float32, jnp.bfloat16
VM = pl.BlockSpec(memory_space=pltpu.VMEM)
SM = pl.BlockSpec(memory_space=pltpu.SMEM)
HB = pl.BlockSpec(memory_space=pltpu.HBM)

L_P, L_LQ, L_Q, L_CQ, L_CQL, L_CP, L_GQ, L_GP = range(8)
PK = 40


def shape(*dims, dtype=F32):
    return jax.ShapeDtypeStruct(dims, dtype)


def iota(dims, axis):
    return lax.broadcasted_iota(jnp.int32, dims, axis)


def fiota(dims, axis):
    return iota(dims, axis).astype(F32)


class Rates:
    def __init__(self, par, level):
        self.a1, self.a2 = par[0, level], par[1, level]
        self.t1, self.c1 = self.decay(self.a1)
        self.t2, self.c2 = self.decay(self.a2)

    def decay(self, a):
        a = jnp.full((1, LN), 1.0, F32) * a
        half = 0.5 / jnp.sqrt(a)
        theta = 2.0 * jnp.log1p(half + half * half / (1.0 + jnp.sqrt(1.0 + half * half)))
        return theta, 1.0 / jnp.sqrt(1.0 + 4.0 * a)


def position():
    return lax.axis_index("lat").astype(F32), lax.axis_index("lon").astype(F32)


def split3(x):
    high = x.astype(BF16)
    rest = x - high.astype(F32)
    mid = rest.astype(BF16)
    return high, mid, (rest - mid.astype(F32)).astype(BF16)


def dot(x, y):
    return jnp.dot(x, y, preferred_element_type=F32)


def tables_kernel(par, after, wt, kt, et, lt, el):
    i_pos, _ = position()
    for l in range(LEV):
        r = Rates(par, l)
        dist = jnp.abs(fiota((LN, LN), 0) - fiota((LN, LN), 1))
        for i, piece in enumerate(split3(r.c1 * jnp.exp(-r.t1 * dist))):
            kt[l, i] = piece
        lane = iota((LN, LN), 1)
        row = fiota((LN, LN), 0)
        slot = lane % 32
        rising = ((lane < 96) & (slot >= 16)) | (lane == 97)
        base = jnp.exp(-r.t1 * jnp.where(rising, row, (LN - 1) - row))

        def weights(k):
            pick = jnp.where((lane < 96) & (slot % 16 == k), 1.0, 0.0)
            pick = jnp.where(lane == 96, jnp.exp(-r.t1 * jnp.full((LN, LN), float(LN * (KT - 1 - k)), F32)), pick)
            pick = jnp.where(lane == 97, jnp.exp(-r.t1 * jnp.full((LN, LN), float(LN * k), F32)), pick)
            for i, piece in enumerate(split3(base * pick)):
                wt[l, k, i] = piece

        for k in range(KT):
            weights(k)
        slot = iota((32, LN), 0)
        col = fiota((32, LN), 1)
        own = (slot % 16).astype(F32)
        for k in range(KT):
            gap = jnp.where(slot < 16, k - own, own - k)
            power = (gap - 1) * LN + jnp.where(slot < 16, col + 1, LN - col)
            value = jnp.where(gap > 0, r.c1 * jnp.exp(-r.t1 * jnp.maximum(power, 0.0)), 0.0)
            high, mid, low = split3(value)
            zero = jnp.zeros_like(high)
            et[l, :, pl.ds(k * LN, LN)] = jnp.concatenate([high, mid, low, zero, high, mid, high, zero], axis=0)
        lane_f = fiota((SS, LN), 1)
        for k in range(KT):
            el[l, 0, k] = r.c1 * jnp.exp(-r.t1 * (k * LN + lane_f + 1.0))
            el[l, 1, k] = r.c1 * jnp.exp(-r.t1 * (COLS - k * LN - lane_f))
        sub = fiota((SS, LN), 0)
        scale = r.c2 / (1.0 - jnp.exp(jnp.full((SS, LN), -2.0 * (NLAT + 1), F32) * r.t2))
        for t in range(TT):
            local = sub * TT + t
            index = local + i_pos * ROWS
            p = 1.0 - jnp.exp(-2.0 * r.t2 * (index + 1.0))
            q = 1.0 - jnp.exp(-2.0 * r.t2 * (NLAT - index))
            lt[l, L_P, t] = p
            lt[l, L_Q, t] = q
            lt[l, L_LQ, t] = q * jnp.exp(jnp.full((SS, LN), -float(t), F32) * r.t2)
            lt[l, L_CQ, t] = scale * q
            lt[l, L_CQL, t] = scale * q * jnp.exp(jnp.full((SS, LN), -float(t + 1), F32) * r.t2)
            lt[l, L_CP, t] = scale * p
            lt[l, L_GQ, t] = scale * q * jnp.exp(-r.t2 * (local + 1.0))
            lt[l, L_GP, t] = scale * p * jnp.exp(-r.t2 * (ROWS - local))


def move_kernel(u_hbm, m_hbm, k_hbm, ul, ml, kl, done, su, sm, sk, sem):
    done[...] = jnp.zeros((SS, LN), F32)
    copies = []
    for l in range(LEV):
        copies.append([pltpu.make_async_copy(u_hbm.at[l, :, pl.ds(k * LN, LN)], su.at[l, k], sem.at[l]) for k in range(KT)])
    for l in range(LEV):
        copies.append([pltpu.make_async_copy(m_hbm.at[l, :, pl.ds(k * LN, LN)], sm.at[l, k], sem.at[2 + l]) for k in range(KT)])
    copies.append([pltpu.make_async_copy(k_hbm.at[:, pl.ds(k * LN, LN)], sk.at[k], sem.at[4]) for k in range(KT)])
    for group in copies:
        for c in group:
            c.start()
    for c in copies[4]:
        c.wait()
    for k in range(KT):
        for t in range(TT):
            kl[k, t] = sk[k, pl.ds(t, SS, stride=TT), :].astype(F32)
    for l in range(LEV):
        for c in copies[l]:
            c.wait()
        for k in range(KT):
            for t in range(TT):
                ul[l, k, t] = su[l, k, pl.ds(t, SS, stride=TT), :]
        for c in copies[2 + l]:
            c.wait()
        for k in range(KT):
            for t in range(TT):
                ml[l, k, t] = sm[l, k, pl.ds(t, SS, stride=TT), :]


def turned(tiles, ext):
    lane = iota((SS, LN), 1)
    at_end, at_start = lane == LN - 1, lane == 0
    zero = jnp.zeros((SS, LN), F32)
    before = zero if ext is None else ext
    right = pltpu.roll(tiles(0), LN - 1, 1)
    for k in range(KT):
        if k + 1 < KT:
            beyond = pltpu.roll(tiles(k + 1), LN - 1, 1)
        else:
            beyond = zero if ext is None else pltpu.roll(ext, LN - 2, 1)
        left = pltpu.roll(tiles(k), 1, 1)
        yield jnp.where(at_end, beyond, right), jnp.where(at_start, before, left)
        right, before = beyond, left


def north_of(last, halo):
    return jnp.where(iota(last.shape, last.ndim - 2) == 0, halo, pltpu.roll(last, 1, last.ndim - 2))


def south_of(first, halo):
    return jnp.where(iota(first.shape, first.ndim - 2) == SS - 1, halo, pltpu.roll(first, SS - 1, first.ndim - 2))


def down_scan(x, t2):
    sub = iota(x.shape, x.ndim - 2)
    x = jnp.where(sub >= 1, pltpu.roll(x, 1, x.ndim - 2), 0.0)
    for step in (1, 2, 4):
        factor = jnp.exp(jnp.full((SS, LN), -float(TT * step), F32) * t2)
        x = x + factor * jnp.where(sub >= step, pltpu.roll(x, step, x.ndim - 2), 0.0)
    return x


def up_scan(x, t2):
    sub = iota(x.shape, x.ndim - 2)
    x = jnp.where(sub < SS - 1, pltpu.roll(x, SS - 1, x.ndim - 2), 0.0)
    for step in (1, 2, 4):
        factor = jnp.exp(jnp.full((SS, LN), -float(TT * step), F32) * t2)
        x = x + factor * jnp.where(sub < SS - step, pltpu.roll(x, SS - step, x.ndim - 2), 0.0)
    return x


def chunk_ends(last, acc, t2):
    carry_down = down_scan(last, t2)
    carry_up = up_scan(acc, t2)
    step = jnp.exp(jnp.full((SS, LN), -float(TT), F32) * t2)
    phi = (last + step * carry_down)[..., SS - 1 : SS, :]
    psi = (acc + step * carry_up)[..., 0:1, :]
    return carry_down, carry_up, jnp.broadcast_to(phi, last.shape), jnp.broadcast_to(psi, last.shape)


def lam2(t2):
    return jnp.exp(jnp.full((SS, LN), -1.0, F32) * t2)


def local_solve(par, qs, xs, ss, wt, kt, et, lt, zl, phi, with_p):
    sums = []
    for l in range(LEV):
        r = Rates(par, l)

        ab = jnp.zeros((ROWS, LN), F32)
        for k in range(KT):
            high, mid, low = split3(qs[l, k].reshape(ROWS, LN))
            lhs = jnp.concatenate([high, mid, low, high, high, mid], axis=1)
            pieces = [jnp.concatenate([kt[l, i], wt[l, k, i]], axis=1) for i in (0, 0, 0, 2, 1, 1)]
            both = dot(lhs, jnp.concatenate(pieces, axis=0))
            x = both[:, :LN].reshape(TT, SS, LN)
            xs[l, k] = xs[l, k] + x if with_p else x
            ab = ab + both[:, LN:]
        sums.append(ab)
        high, mid, low = split3(ab)
        lane = iota((ROWS, LN), 1)
        second = jnp.where(lane < 64, mid.astype(F32), low.astype(F32)).astype(BF16)
        lhs = jnp.concatenate([high, second], axis=1)
        for k in range(0, KT, 2):
            fix = dot(lhs, et[l, :, pl.ds(k * LN, 2 * LN)])
            xs[l, k] += fix[:, :LN].reshape(TT, SS, LN)
            xs[l, k + 1] += fix[:, LN:].reshape(TT, SS, LN)

        lam = lam2(r.t2)

        def down(t, carry):
            s, acc = carry
            x = xs[l, :, t]
            s = lam * s + lt[l, L_P, t] * x
            ss[:, t] = s
            return s, acc + lt[l, L_LQ, t] * x

        zero = jnp.zeros((KT, SS, LN), F32)
        last, acc = zero, zero
        for t in range(TT):
            last, acc = down(t, (last, acc))
        carry_down, carry_up, phi_l, psi_l = chunk_ends(last, acc, r.t2)
        phi[l, 0] = phi_l
        phi[l, 1] = psi_l

        def up(i, u):
            t = TT - 1 - i
            zl[l, :, t] = lt[l, L_CQ, t] * ss[:, t] + lt[l, L_CQL, t] * carry_down + lt[l, L_CP, t] * u
            return lam * (u + lt[l, L_Q, t] * xs[l, :, t])

        u = lam * carry_up
        for i in range(TT):
            u = up(i, u)
    return sums


def explicit(r, l, t, before, here, after, ext_here, ext_diff, ml, kl, qs, xs):
    here = [here(k) for k in range(KT)]
    around = []
    diff = []
    for k in range(KT):
        up, down = before(k), after(k)
        around.append(down + up - 2.0 * here[k])
        diff.append(down - up)
    flat = zip(turned(lambda k: here[k], ext_here), turned(lambda k: diff[k], ext_diff))
    for k, ((east, west), (diff_east, diff_west)) in enumerate(flat):
        lon = east + west - 2.0 * here[k]
        inner = here[k] + ml[l, k, t] * (diff_east - diff_west) + (2.0 * r.a1) * lon + (2.0 * r.a2) * around[k]
        qs[l, k, t] = kl[k, t] * inner - r.a1 * lon
        xs[l, k, t] = -r.a2 * around[k]


def end_columns(first, last):
    lane = iota((ROWS, LN), 1)
    turned = jnp.where(lane < 64, first, last).T
    return turned[0:1], turned[LN - 1 : LN]


def first_kernel(par, ul, ml, kl, north, south, wt, kt, et, lt, zl, phi, msg, uh, kh, qs, xs, ss):
    def spread(ref, row):
        return jnp.stack([jnp.broadcast_to(ref[row, k : k + 1, :], (SS, LN)) for k in range(KT)])

    for side, ref in ((0, north), (1, south)):
        kh[side, :KT] = spread(ref, 2)
    for l in range(LEV):
        r = Rates(par, l)
        uh[l, 0, :KT] = spread(north, l)
        uh[l, 1, :KT] = spread(south, l)

        for t in range(TT):
            if t == 0:
                before = lambda k: north_of(ul[l, k, TT - 1], uh[l, 0, k])
            else:
                before = lambda k, t=t: ul[l, k, t - 1]
            if t == TT - 1:
                after = lambda k: south_of(ul[l, k, 0], uh[l, 1, k])
            else:
                after = lambda k, t=t: ul[l, k, t + 1]
            explicit(r, l, t, before, lambda k, t=t: ul[l, k, t], after, None, None, ml, kl, qs, xs)
    sums = local_solve(par, qs, xs, ss, wt, kt, et, lt, zl, phi, True)
    parts = []
    for l in range(LEV):
        parts.append(sums[l].T[96:98])
    for l in range(LEV):
        parts.extend(end_columns(ul[l, 0].reshape(ROWS, LN), ul[l, KT - 1].reshape(ROWS, LN)))
    for l in range(LEV):
        parts.extend(end_columns(ml[l, 0].reshape(ROWS, LN), ml[l, KT - 1].reshape(ROWS, LN)))
    parts.extend(end_columns(kl[0].reshape(ROWS, LN), kl[KT - 1].reshape(ROWS, LN)))
    lane = iota((1, LN), 1)
    for row in range(3):
        n0, s0 = north[row, 0:1, :], south[row, 0:1, :]
        n1, s1 = north[row, KT - 1 : KT, :], south[row, KT - 1 : KT, :]
        parts.append(jnp.where(lane == 0, n0, pltpu.roll(s0, 1, 1)))
        parts.append(jnp.where(lane == LN - 1, n1, pltpu.roll(s1, LN - 1, 1)))
    parts.append(jnp.zeros((4, LN), F32))
    block = jnp.concatenate(parts, axis=0)
    for j in range(NLON_DEV):
        msg[j] = block


def row_after(x, halo):
    lane = iota(x.shape, 1)
    y = jnp.where(lane >= LN - SS, pltpu.roll(x, LN - SS - 1, 1), pltpu.roll(x, LN - SS, 1))
    return jnp.where(lane == LN - 1, halo, y)


def row_before(x, halo):
    lane = iota(x.shape, 1)
    y = jnp.where(lane < SS, pltpu.roll(x, SS + 1, 1), pltpu.roll(x, SS, 1))
    return jnp.where(lane == 0, halo, y)


def lane_value(x, index):
    return jnp.sum(jnp.where(iota(x.shape, x.ndim - 1) == index, x, 0.0), axis=-1, keepdims=True)


def as_tile(rows):
    count = sum(r.shape[0] for r in rows)
    return jnp.concatenate(rows + [jnp.zeros((LN - count, LN), F32)], axis=0).T.reshape(TT, SS, LN)


def carry_kernel(first, *refs):
    if first:
        par, got, phi, lt, el, out, pack, ze, ux, kx, uhx, khx = refs
    else:
        par, got, phi, px, lt, el, out, pack, ze = refs
    i_pos, j_pos = position()
    peer = fiota((NLON_DEV, LN), 0)
    mine = peer == j_pos
    fluxes = []
    ext = []
    if first:
        kw = pltpu.roll(got[:, 13, :], 1, 0)
        ke = pltpu.roll(got[:, 12, :], NLON_DEV - 1, 0)
        kw_end = pltpu.roll(got[:, 19, :], 1, 0)
        ke_end = pltpu.roll(got[:, 18, :], NLON_DEV - 1, 0)

        def own(x):
            return jnp.sum(jnp.where(mine, x, 0.0), axis=0, keepdims=True)

        def corners(west_end, east_end):
            lane = iota((1, LN), 1)
            w, e = own(west_end), own(east_end)
            w_n, w_s = lane_value(w, LN - 1), lane_value(w, LN - 2)
            e_n, e_s = lane_value(e, 0), lane_value(e, 1)
            pick = lambda a, b: jnp.broadcast_to(jnp.where(lane == 0, a, jnp.where(lane == 1, b, 0.0)), (SS, LN))
            return pick(w_n, e_n), pick(w_s, e_s)

        khx[0], khx[1] = corners(kw_end, ke_end)
        kx[...] = as_tile([own(kw), own(ke)])
    for l in range(LEV):
        r = Rates(par, l)
        a, b = got[:, 2 * l, :], got[:, 2 * l + 1, :]
        one = jnp.full((NLON_DEV, LN), 1.0, F32)
        if first:
            uw = pltpu.roll(got[:, 5 + 2 * l, :], 1, 0)
            ue = pltpu.roll(got[:, 4 + 2 * l, :], NLON_DEV - 1, 0)
            uw_end = pltpu.roll(got[:, 15 + 2 * l, :], 1, 0)
            ue_end = pltpu.roll(got[:, 14 + 2 * l, :], NLON_DEV - 1, 0)
            w_up = row_before(uw, jnp.sum(jnp.where(iota(uw.shape, 1) == LN - 1, uw_end, 0.0), axis=1, keepdims=True))
            w_dn = row_after(uw, jnp.sum(jnp.where(iota(uw.shape, 1) == LN - 2, uw_end, 0.0), axis=1, keepdims=True))
            e_up = row_before(ue, jnp.sum(jnp.where(iota(ue.shape, 1) == 0, ue_end, 0.0), axis=1, keepdims=True))
            e_dn = row_after(ue, jnp.sum(jnp.where(iota(ue.shape, 1) == 1, ue_end, 0.0), axis=1, keepdims=True))
            m0, mn, k0, kn = got[:, 8 + 2 * l, :], got[:, 9 + 2 * l, :], got[:, 12, :], got[:, 13, :]
            h0 = k0 * (m0 * (w_up - w_dn) + 2.0 * r.a1 * uw) - r.a1 * uw
            hn = kn * (mn * (e_dn - e_up) + 2.0 * r.a1 * ue) - r.a1 * ue
            far = jnp.exp(-(COLS - 1.0) * r.t1 * one)
            a = a + far * h0 + hn
            b = b + h0 + far * hn
        whole = 1.0 - jnp.exp(-float(NLON) * r.t1 * one)
        back = j_pos - peer - 1.0
        back = jnp.where(back < 0, back + NLON_DEV, back)
        ahead = peer - j_pos - 1.0
        ahead = jnp.where(ahead < 0, ahead + NLON_DEV, ahead)
        left = jnp.sum(a * (jnp.exp(-r.t1 * COLS * back) / whole), axis=0, keepdims=True)
        right = jnp.sum(b * (jnp.exp(-r.t1 * COLS * ahead) / whole), axis=0, keepdims=True)
        a = jnp.sum(jnp.where(mine, a, 0.0), axis=0, keepdims=True)
        b = jnp.sum(jnp.where(mine, b, 0.0), axis=0, keepdims=True)
        lam = jnp.exp(-r.t1 * jnp.full((1, LN), 1.0, F32))
        far = jnp.exp(-(COLS + 1.0) * r.t1 * jnp.full((1, LN), 1.0, F32))
        xw = r.c1 * (left + lam * b + far * right)
        xe = r.c1 * (right + lam * a + far * left)
        if first:
            pw = -r.a2 * (w_dn + w_up - 2.0 * uw)
            pe = -r.a2 * (e_dn + e_up - 2.0 * ue)
            xw = xw + own(pw)
            xe = xe + own(pe)
            left = left + own(h0) / lam
            right = right + own(hn) / lam
            ux[l] = as_tile([own(uw), own(ue)])
            uhx[l, 0], uhx[l, 1] = corners(uw_end, ue_end)
        x = as_tile([xw, xe, left, right])
        if not first:
            x = x + px[l]
        ext.append(x)
    lams = [lam2(Rates(par, l).t2) for l in range(LEV)]
    zero = jnp.zeros((SS, LN), F32)
    state = [zero, zero]
    acc = [zero, zero]
    kept = [[], []]
    for t in range(TT):
        for l in range(LEV):
            state[l] = lams[l] * state[l] + lt[l, L_P, t] * ext[l][t]
            acc[l] = acc[l] + lt[l, L_LQ, t] * ext[l][t]
            kept[l].append(state[l])
    for l in range(LEV):
        r = Rates(par, l)
        carry_down, carry_up, phi_e, psi_e = chunk_ends(state[l], acc[l], r.t2)
        u = lams[l] * carry_up
        for t in range(TT - 1, -1, -1):
            ze[l, t] = lt[l, L_CQ, t] * kept[l][t] + lt[l, L_CQL, t] * carry_down + lt[l, L_CP, t] * u
            u = lams[l] * (u + lt[l, L_Q, t] * ext[l][t])
        pair = []
        for side, flux in ((0, phi_e), (1, psi_e)):
            tiles = phi[l, side] + lane_value(flux, 2) * el[l, 0] + lane_value(flux, 3) * el[l, 1]
            pair.append([tiles[k] for k in range(KT)] + [flux])
        fluxes.append(pair)
    sub = iota((SS, LN), 0)
    packed = []
    for side in (0, 1):
        rows = fluxes[0][side] + fluxes[1][side]
        rows = rows + [zero] * (PK - len(rows))
        vregs = []
        for v in range(PK // SS):
            y = rows[v * SS]
            for j in range(1, SS):
                y = jnp.where(sub == j, rows[v * SS + j], y)
            vregs.append(y)
        packed.append(jnp.concatenate(vregs, axis=0))
        pack[side] = packed[side]
    t2 = level_rows(Rates(par, 0).t2, Rates(par, 1).t2)
    for p in range(NLAT_DEV):
        away = jnp.maximum(jnp.abs(p - i_pos) - 1.0, 0.0)
        factor = jnp.exp(-(ROWS * away) * t2)
        ahead = jnp.full((PK, LN), p - i_pos, F32) > 0
        out[p] = factor * jnp.where(ahead, packed[0], packed[1])


def level_rows(low, high):
    return jnp.where(iota((PK, LN), 0) <= KT, low, high)


def arrive(par, got, pack, tb, vb, hb):
    i_pos, _ = position()
    zero = jnp.zeros((PK, LN), F32)
    above, below = zero, zero
    for p in range(NLAT_DEV):
        side = jnp.full((PK, LN), p - i_pos, F32)
        above = above + jnp.where(side < 0, got[p], 0.0)
        below = below + jnp.where(side > 0, got[p], 0.0)
    t2 = level_rows(Rates(par, 0).t2, Rates(par, 1).t2)
    scale = level_rows(Rates(par, 0).c2, Rates(par, 1).c2) / (1.0 - jnp.exp(-2.0 * (NLAT + 1) * t2))
    lam = jnp.exp(-t2)
    block = jnp.exp(-float(ROWS) * t2)
    start = i_pos * ROWS
    q_n = 1.0 - jnp.exp(-2.0 * t2 * (NLAT + 1.0 - start))
    p_n = 1.0 - jnp.exp(-2.0 * t2 * start)
    q_s = 1.0 - jnp.exp(-2.0 * t2 * (NLAT - ROWS - start))
    p_s = 1.0 - jnp.exp(-2.0 * t2 * (ROWS + 1.0 + start))
    north = scale * (q_n * above + p_n * lam * (pack[1] + block * below))
    south = scale * (q_s * lam * (pack[0] + block * above) + p_s * below)
    for l in range(LEV):
        for k in range(KT + 1):
            at = l * (KT + 1) + k
            wide = lambda x: jnp.broadcast_to(x[at : at + 1], (SS, LN))
            tb[l, k] = wide(above)
            vb[l, k] = wide(below)
            if hb is not None:
                hb[l, 0, k] = wide(north)
                hb[l, 1, k] = wide(south)


def solved_rows(l, zl, ze, el, lt, tb, vb, use, use_extra):
    step = 4
    for start in range(0, TT, step):
        times = range(start, start + step)
        extra = [ze[l, t] for t in times]
        gq = [lt[l, L_GQ, t] for t in times]
        gp = [lt[l, L_GP, t] for t in times]
        z_left = [jnp.broadcast_to(x[:, 2:3], (SS, LN)) for x in extra]
        z_right = [jnp.broadcast_to(x[:, 3:4], (SS, LN)) for x in extra]
        for k in range(KT):
            e_left, e_right, above, below = el[l, 0, k], el[l, 1, k], tb[l, k], vb[l, k]
            for i, t in enumerate(times):
                use(k, t, zl[l, k, t] + e_left * z_left[i] + e_right * z_right[i] + gq[i] * above + gp[i] * below)
        if use_extra is not None:
            above, below = tb[l, KT], vb[l, KT]
            for i, t in enumerate(times):
                use_extra(t, extra[i] + gq[i] * above + gp[i] * below)


def send_sums(sums, msg):
    block = jnp.concatenate([s.T[96:98] for s in sums] + [jnp.zeros((4, LN), F32)], axis=0)
    for j in range(NLON_DEV):
        msg[j] = block


def half_kernel(par, got, pack, zl, ze, ul, ux, uh, uhx, ml, el, wt, kt, et, lt,
                y2, yx, yh, zo, phi, msg, px, tb, vb, vs, qs, xs, ss):
    arrive(par, got, pack, tb, vb, yh)
    for l in range(LEV):
        r = Rates(par, l)

        def use(k, t, own):
            y2[l, k, t] = own
            vs[k, t + 1] = own - ul[l, k, t]

        def use_extra(t, extra):
            yx[l, t] = extra
            vs[KT, t + 1] = extra - ux[l, t]
            px[l, t] = jnp.zeros((SS, LN), F32)

        solved_rows(l, zl, ze, el, lt, tb, vb, use, use_extra)
        for side, edge, at, turn in ((0, TT, 0, north_of), (1, 1, TT + 1, south_of)):
            vs[:KT, at] = turn(vs[:KT, edge], yh[l, side, :KT] - uh[l, side, :KT])
            vs[KT, at] = turn(vs[KT, edge], yh[l, side, KT] - uhx[l, side])

        for t in range(TT):
            diff = [vs[k, t + 2] - vs[k, t] for k in range(KT + 1)]
            for k, (east, west) in enumerate(turned(lambda k: diff[k], diff[KT])):
                qs[l, k, t] = 0.5 * ml[l, k, t] * (east - west)
    send_sums(local_solve(par, qs, xs, ss, wt, kt, et, lt, zo, phi, False), msg)


def step_kernel(par, got, pack, zl, ze, y2, yx, yh, kl, kx, kh, khx, ml, el, wt, kt, et, lt,
                un, unx, unh, unhx, zo, phi, msg, px, tb, vb, hb, vs, qs, xs, ss):
    arrive(par, got, pack, tb, vb, hb)
    for l in range(LEV):
        r = Rates(par, l)

        def use(k, t, own):
            own = kl[k, t] * (own + y2[l, k, t])
            un[l, k, t] = own
            vs[k, t + 1] = own

        def use_extra(t, extra):
            extra = kx[t] * (extra + yx[l, t])
            unx[l, t] = extra
            vs[KT, t + 1] = extra

        solved_rows(l, zl, ze, el, lt, tb, vb, use, use_extra)
        for side, edge, at, turn in ((0, TT, 0, north_of), (1, 1, TT + 1, south_of)):
            halo = kh[side, :KT] * (yh[l, side, :KT] + hb[l, side, :KT])
            halo_x = khx[side] * (yh[l, side, KT] + hb[l, side, KT])
            unh[l, side, :KT] = halo
            unhx[l, side] = halo_x
            vs[:KT, at] = turn(vs[:KT, edge], halo)
            vs[KT, at] = turn(vs[KT, edge], halo_x)

        for t in range(TT):
            before, here, after = vs[KT, t], vs[KT, t + 1], vs[KT, t + 2]
            explicit(r, l, t, lambda k: vs[k, t], lambda k: vs[k, t + 1], lambda k: vs[k, t + 2],
                     here, after - before, ml, kl, qs, xs)
            px[l, t] = jnp.where(iota((SS, LN), 1) < 2, -r.a2 * (after + before - 2.0 * here), 0.0)
    send_sums(local_solve(par, qs, xs, ss, wt, kt, et, lt, zo, phi, True), msg)


def last_kernel(par, got, pack, zl, ze, y2, kl, el, lt, out, tb, vb, zs, os, sem):
    arrive(par, got, pack, tb, vb, None)
    copies = []
    for l in range(LEV):
        for k in range(KT):
            e_left, e_right, above, below = el[l, 0, k], el[l, 1, k], tb[l, k], vb[l, k]
            for t in range(TT):
                if k == 0:
                    extra = ze[l, t]
                    zs[0, t] = jnp.broadcast_to(extra[:, 2:3], (SS, LN))
                    zs[1, t] = jnp.broadcast_to(extra[:, 3:4], (SS, LN))
                z = zl[l, k, t] + e_left * zs[0, t] + e_right * zs[1, t]
                z = z + lt[l, L_GQ, t] * above + lt[l, L_GP, t] * below
                os[l, k, pl.ds(t, SS, stride=TT), :] = kl[k, t] * (z + y2[l, k, t])
            copies.append(pltpu.make_async_copy(os.at[l, k], out.at[l, :, pl.ds(k * LN, LN)], sem.at[l]))
            copies[-1].start()
    for c in copies:
        c.wait()


FIELD = (LEV, KT, TT, SS, LN)
EXTRA = (LEV, TT, SS, LN)
HALO = (LEV, 2, KT + 1, SS, LN)
FLUX = (LEV, 2, KT, SS, LN)


def call(kernel, outs, ins, scratch=(), out_specs=None, in_specs=None, limit=10):
    return pl.pallas_call(
        kernel,
        out_shape=outs,
        in_specs=in_specs or [SM] + [VM] * (len(ins) - 1),
        out_specs=out_specs or [VM] * len(outs),
        scratch_shapes=list(scratch),
        compiler_params=pltpu.CompilerParams(vmem_limit_bytes=limit * 1024 * 1024),
    )(*ins)


def vmem(*dims):
    return pltpu.VMEM(dims, F32)


def rows_kernel(u_hbm, k_hbm, one, two, su, sk, sem):
    copies = []
    for side, at in ((0, 0), (1, ROWS - SS)):
        for l in range(LEV):
            copies.append(pltpu.make_async_copy(u_hbm.at[l, pl.ds(at, SS)], su.at[l, side], sem.at[l, side]))
        copies.append(pltpu.make_async_copy(k_hbm.at[pl.ds(at, SS)], sk.at[side], sem.at[LEV, side]))
    for c in copies:
        c.start()
    for c in copies:
        c.wait()
    even = jnp.full((1, LN), lax.axis_index("lat") % 2, jnp.int32) == 0
    for k in range(KT):
        at = pl.ds(k * LN, LN)
        for row in range(LEV + 1):
            if row < LEV:
                first, last = su[row, 0, 0:1, at], su[row, 1, SS - 1 : SS, at]
            else:
                first, last = sk[0, 0:1, at].astype(F32), sk[1, SS - 1 : SS, at].astype(F32)
            one[row, k : k + 1, :] = jnp.where(even, last, first)
            two[row, k : k + 1, :] = jnp.where(even, first, last)


def halo_rows(ensemble, mask):
    one, two = call(
        rows_kernel,
        [shape(LEV + 1, KT, LN), shape(LEV + 1, KT, LN)],
        [ensemble[:, 0], mask],
        [vmem(LEV, 2, SS, COLS), pltpu.VMEM((2, SS, COLS), jnp.int32), pltpu.SemaphoreType.DMA((LEV + 1, 2))],
        in_specs=[HB, HB],
        limit=57,
    )
    pairs = [(i, i + 1) for i in range(0, NLAT_DEV, 2)]
    odd_pairs = [(i, i + 1) for i in range(1, NLAT_DEV - 1, 2)]
    both = lambda edges: edges + [(j, i) for i, j in edges]
    one = lax.ppermute(one, "lat", both(pairs))
    two = lax.ppermute(two, "lat", both(odd_pairs))
    even = lax.axis_index("lat") % 2 == 0
    return jnp.where(even, two, one), jnp.where(even, one, two)


def exchange(values, axis):
    return lax.all_to_all(values, axis, split_axis=0, concat_axis=0, tiled=True)


def shards(ensemble, cross_mix, sea_mask, level_rates, panel_inverse, reduced_lon, reduced_lat):
    par = level_rates
    north, south = halo_rows(ensemble, sea_mask)
    work = [vmem(*FIELD), vmem(*FIELD), vmem(KT, TT, SS, LN)]
    carries = [vmem(LEV, KT + 1, SS, LN), vmem(LEV, KT + 1, SS, LN)]
    diffs = vmem(KT + 1, TT + 2, SS, LN)
    ul, ml, kl, done = call(
        move_kernel,
        [shape(*FIELD), shape(*FIELD), shape(KT, TT, SS, LN), shape(SS, LN)],
        [ensemble[:, 0], cross_mix, sea_mask],
        [vmem(LEV, KT, ROWS, LN), vmem(LEV, KT, ROWS, LN), pltpu.VMEM((KT, ROWS, LN), jnp.int32),
         pltpu.SemaphoreType.DMA((5,))],
        in_specs=[HB, HB, HB],
        limit=45,
    )
    wt, kt, et, lt, el = call(
        tables_kernel,
        [shape(LEV, KT, 3, LN, LN, dtype=BF16), shape(LEV, 3, LN, LN, dtype=BF16),
         shape(LEV, 2 * LN, COLS, dtype=BF16), shape(LEV, 8, TT, SS, LN), shape(LEV, 2, KT, SS, LN)],
        [par, done],
    )
    mats = [wt, kt, et, lt]
    solve_out = [shape(*FIELD), shape(*FLUX), shape(NLON_DEV, 8, LN)]
    carry_out = [shape(NLAT_DEV, PK, LN), shape(2, PK, LN), shape(*EXTRA)]
    zl, phi, msg, uh, kh = call(
        first_kernel,
        [shape(*FIELD), shape(*FLUX), shape(NLON_DEV, 24, LN), shape(*HALO), shape(2, KT + 1, SS, LN)],
        [par, ul, ml, kl, north, south] + mats,
        work,
    )
    got = exchange(msg, "lon")
    out, pack, ze, ux, kx, uhx, khx = call(
        functools.partial(carry_kernel, True),
        carry_out + [shape(*EXTRA), shape(TT, SS, LN), shape(LEV, 2, SS, LN), shape(2, SS, LN)],
        [par, got, phi, lt, el],
    )
    for step in range(2):
        got = exchange(out, "lat")
        y2, yx, yh, zl, phi, msg, px = call(
            half_kernel,
            [shape(*FIELD), shape(*EXTRA), shape(*HALO)] + solve_out + [shape(*EXTRA)],
            [par, got, pack, zl, ze, ul, ux, uh, uhx, ml, el] + mats,
            carries + [diffs] + work,
        )
        got = exchange(msg, "lon")
        out, pack, ze = call(functools.partial(carry_kernel, False), carry_out, [par, got, phi, px, lt, el])
        got = exchange(out, "lat")
        if step == 1:
            break
        ul, ux, uh, uhx, zl, phi, msg, px = call(
            step_kernel,
            [shape(*FIELD), shape(*EXTRA), shape(*HALO), shape(LEV, 2, SS, LN)] + solve_out + [shape(*EXTRA)],
            [par, got, pack, zl, ze, y2, yx, yh, kl, kx, kh, khx, ml, el] + mats,
            carries + [vmem(*HALO), diffs] + work,
        )
        got = exchange(msg, "lon")
        out, pack, ze = call(functools.partial(carry_kernel, False), carry_out, [par, got, phi, px, lt, el])
    (final,) = call(
        last_kernel,
        [shape(LEV, ROWS, COLS)],
        [par, got, pack, zl, ze, y2, kl, el, lt],
        carries + [vmem(2, TT, SS, LN), vmem(LEV, KT, ROWS, LN), pltpu.SemaphoreType.DMA((LEV,))],
        out_specs=[HB],
    )
    return final[:, None]


def solution(mesh):
    in_specs = (
        P(None, None, "lat", "lon"),
        P(None, "lat", "lon"),
        P("lat", "lon"),
        P(),
        P(),
        P(),
        P(),
    )
    out_specs = P(None, None, "lat", "lon")
    return jax.shard_map(shards, mesh=mesh, in_specs=in_specs, out_specs=out_specs, check_vma=False)
```

```python
import functools

import jax
import jax.numpy as jnp
from jax import lax
from jax.experimental import pallas as pl
from jax.experimental.pallas import tpu as pltpu
from jax.sharding import PartitionSpec as P

LEV, ROWS, COLS = 2, 128, 2048
KT, TT, SS, LN = 16, 16, 8, 128
NLAT_DEV, NLON_DEV = 16, 8
NLAT, NLON = ROWS * NLAT_DEV, COLS * NLON_DEV
F32, BF16 = jnp.float32, jnp.bfloat16
VM = pl.BlockSpec(memory_space=pltpu.VMEM)
SM = pl.BlockSpec(memory_space=pltpu.SMEM)
HB = pl.BlockSpec(memory_space=pltpu.HBM)

L_P, L_LQ, L_Q, L_CQ, L_CQL, L_CP, L_GQ, L_GP = range(8)
PK = 40


def shape(*dims, dtype=F32):
    return jax.ShapeDtypeStruct(dims, dtype)


def iota(dims, axis):
    return lax.broadcasted_iota(jnp.int32, dims, axis)


def fiota(dims, axis):
    return iota(dims, axis).astype(F32)


class Rates:
    def __init__(self, par, level):
        self.a1, self.a2 = par[0, level], par[1, level]
        self.t1, self.c1 = self.decay(self.a1)
        self.t2, self.c2 = self.decay(self.a2)

    def decay(self, a):
        a = jnp.full((1, LN), 1.0, F32) * a
        half = 0.5 / jnp.sqrt(a)
        theta = 2.0 * jnp.log1p(half + half * half / (1.0 + jnp.sqrt(1.0 + half * half)))
        return theta, 1.0 / jnp.sqrt(1.0 + 4.0 * a)


def position():
    return lax.axis_index("lat").astype(F32), lax.axis_index("lon").astype(F32)


def split3(x):
    high = x.astype(BF16)
    rest = x - high.astype(F32)
    mid = rest.astype(BF16)
    return high, mid, (rest - mid.astype(F32)).astype(BF16)


def dot(x, y):
    return jnp.dot(x, y, preferred_element_type=F32)


def tables_kernel(par, after, wt, kt, et, lt, el):
    i_pos, _ = position()
    for l in range(LEV):
        r = Rates(par, l)
        dist = jnp.abs(fiota((LN, LN), 0) - fiota((LN, LN), 1))
        for i, piece in enumerate(split3(r.c1 * jnp.exp(-r.t1 * dist))):
            kt[l, i] = piece
        lane = iota((LN, LN), 1)
        row = fiota((LN, LN), 0)
        slot = lane % 32
        rising = ((lane < 96) & (slot >= 16)) | (lane == 97)
        base = jnp.exp(-r.t1 * jnp.where(rising, row, (LN - 1) - row))

        def weights(k):
            pick = jnp.where((lane < 96) & (slot % 16 == k), 1.0, 0.0)
            pick = jnp.where(lane == 96, jnp.exp(-r.t1 * jnp.full((LN, LN), float(LN * (KT - 1 - k)), F32)), pick)
            pick = jnp.where(lane == 97, jnp.exp(-r.t1 * jnp.full((LN, LN), float(LN * k), F32)), pick)
            for i, piece in enumerate(split3(base * pick)):
                wt[l, k, i] = piece

        for k in range(KT):
            weights(k)
        slot = iota((32, LN), 0)
        col = fiota((32, LN), 1)
        own = (slot % 16).astype(F32)
        for k in range(KT):
            gap = jnp.where(slot < 16, k - own, own - k)
            power = (gap - 1) * LN + jnp.where(slot < 16, col + 1, LN - col)
            value = jnp.where(gap > 0, r.c1 * jnp.exp(-r.t1 * jnp.maximum(power, 0.0)), 0.0)
            high, mid, low = split3(value)
            zero = jnp.zeros_like(high)
            et[l, :, pl.ds(k * LN, LN)] = jnp.concatenate([high, mid, low, zero, high, mid, high, zero], axis=0)
        lane_f = fiota((SS, LN), 1)
        for k in range(KT):
            el[l, 0, k] = r.c1 * jnp.exp(-r.t1 * (k * LN + lane_f + 1.0))
            el[l, 1, k] = r.c1 * jnp.exp(-r.t1 * (COLS - k * LN - lane_f))
        sub = fiota((SS, LN), 0)
        scale = r.c2 / (1.0 - jnp.exp(jnp.full((SS, LN), -2.0 * (NLAT + 1), F32) * r.t2))
        for t in range(TT):
            local = sub * TT + t
            index = local + i_pos * ROWS
            p = 1.0 - jnp.exp(-2.0 * r.t2 * (index + 1.0))
            q = 1.0 - jnp.exp(-2.0 * r.t2 * (NLAT - index))
            lt[l, L_P, t] = p
            lt[l, L_Q, t] = q
            lt[l, L_LQ, t] = q * jnp.exp(jnp.full((SS, LN), -float(t), F32) * r.t2)
            lt[l, L_CQ, t] = scale * q
            lt[l, L_CQL, t] = scale * q * jnp.exp(jnp.full((SS, LN), -float(t + 1), F32) * r.t2)
            lt[l, L_CP, t] = scale * p
            lt[l, L_GQ, t] = scale * q * jnp.exp(-r.t2 * (local + 1.0))
            lt[l, L_GP, t] = scale * p * jnp.exp(-r.t2 * (ROWS - local))


def move_kernel(u_hbm, m_hbm, k_hbm, ul, ml, kl, done, su, sm, sk, sem):
    done[...] = jnp.zeros((SS, LN), F32)
    copies = []
    for l in range(LEV):
        copies.append([pltpu.make_async_copy(u_hbm.at[l, :, pl.ds(k * LN, LN)], su.at[l, k], sem.at[l]) for k in range(KT)])
    for l in range(LEV):
        copies.append([pltpu.make_async_copy(m_hbm.at[l, :, pl.ds(k * LN, LN)], sm.at[l, k], sem.at[2 + l]) for k in range(KT)])
    copies.append([pltpu.make_async_copy(k_hbm.at[:, pl.ds(k * LN, LN)], sk.at[k], sem.at[4]) for k in range(KT)])
    for group in copies:
        for c in group:
            c.start()
    for c in copies[4]:
        c.wait()
    for k in range(KT):
        for t in range(TT):
            kl[k, t] = sk[k, pl.ds(t, SS, stride=TT), :].astype(F32)
    for l in range(LEV):
        for c in copies[l]:
            c.wait()
        for k in range(KT):
            for t in range(TT):
                ul[l, k, t] = su[l, k, pl.ds(t, SS, stride=TT), :]
        for c in copies[2 + l]:
            c.wait()
        for k in range(KT):
            for t in range(TT):
                ml[l, k, t] = sm[l, k, pl.ds(t, SS, stride=TT), :]


def turned(tiles, ext):
    lane = iota((SS, LN), 1)
    at_end, at_start = lane == LN - 1, lane == 0
    zero = jnp.zeros((SS, LN), F32)
    before = zero if ext is None else ext
    right = pltpu.roll(tiles(0), LN - 1, 1)
    for k in range(KT):
        if k + 1 < KT:
            beyond = pltpu.roll(tiles(k + 1), LN - 1, 1)
        else:
            beyond = zero if ext is None else pltpu.roll(ext, LN - 2, 1)
        left = pltpu.roll(tiles(k), 1, 1)
        yield jnp.where(at_end, beyond, right), jnp.where(at_start, before, left)
        right, before = beyond, left


def north_of(last, halo):
    return jnp.where(iota(last.shape, last.ndim - 2) == 0, halo, pltpu.roll(last, 1, last.ndim - 2))


def south_of(first, halo):
    return jnp.where(iota(first.shape, first.ndim - 2) == SS - 1, halo, pltpu.roll(first, SS - 1, first.ndim - 2))


def down_scan(x, t2):
    sub = iota(x.shape, x.ndim - 2)
    x = jnp.where(sub >= 1, pltpu.roll(x, 1, x.ndim - 2), 0.0)
    for step in (1, 2, 4):
        factor = jnp.exp(jnp.full((SS, LN), -float(TT * step), F32) * t2)
        x = x + factor * jnp.where(sub >= step, pltpu.roll(x, step, x.ndim - 2), 0.0)
    return x


def up_scan(x, t2):
    sub = iota(x.shape, x.ndim - 2)
    x = jnp.where(sub < SS - 1, pltpu.roll(x, SS - 1, x.ndim - 2), 0.0)
    for step in (1, 2, 4):
        factor = jnp.exp(jnp.full((SS, LN), -float(TT * step), F32) * t2)
        x = x + factor * jnp.where(sub < SS - step, pltpu.roll(x, SS - step, x.ndim - 2), 0.0)
    return x


def chunk_ends(last, acc, t2):
    carry_down = down_scan(last, t2)
    carry_up = up_scan(acc, t2)
    step = jnp.exp(jnp.full((SS, LN), -float(TT), F32) * t2)
    phi = (last + step * carry_down)[..., SS - 1 : SS, :]
    psi = (acc + step * carry_up)[..., 0:1, :]
    return carry_down, carry_up, jnp.broadcast_to(phi, last.shape), jnp.broadcast_to(psi, last.shape)


def lam2(t2):
    return jnp.exp(jnp.full((SS, LN), -1.0, F32) * t2)


def local_solve(par, qs, xs, ss, wt, kt, et, lt, zl, phi, with_p):
    sums = []
    for l in range(LEV):
        r = Rates(par, l)

        ab = jnp.zeros((ROWS, LN), F32)
        for k in range(KT):
            high, mid, low = split3(qs[l, k].reshape(ROWS, LN))
            lhs = jnp.concatenate([high, mid, low, high, high, mid], axis=1)
            pieces = [jnp.concatenate([kt[l, i], wt[l, k, i]], axis=1) for i in (0, 0, 0, 2, 1, 1)]
            both = dot(lhs, jnp.concatenate(pieces, axis=0))
            x = both[:, :LN].reshape(TT, SS, LN)
            xs[l, k] = xs[l, k] + x if with_p else x
            ab = ab + both[:, LN:]
        sums.append(ab)
        high, mid, low = split3(ab)
        lane = iota((ROWS, LN), 1)
        second = jnp.where(lane < 64, mid.astype(F32), low.astype(F32)).astype(BF16)
        lhs = jnp.concatenate([high, second], axis=1)
        lam = lam2(r.t2)
        zero = jnp.zeros((SS, LN), F32)
        for pair in range(0, KT, 2):
            fix = dot(lhs, et[l, :, pl.ds(pair * LN, 2 * LN)])
            for k in (pair, pair + 1):
                at = (k - pair) * LN
                x = xs[l, k] + fix[:, at : at + LN].reshape(TT, SS, LN)
                last, acc, kept = zero, zero, []
                for t in range(TT):
                    last = lam * last + lt[l, L_P, t] * x[t]
                    acc = acc + lt[l, L_LQ, t] * x[t]
                    kept.append(last)
                carry_down, carry_up, phi[l, 0, k], phi[l, 1, k] = chunk_ends(last, acc, r.t2)
                u = lam * carry_up
                for t in range(TT - 1, -1, -1):
                    zl[l, k, t] = lt[l, L_CQ, t] * kept[t] + lt[l, L_CQL, t] * carry_down + lt[l, L_CP, t] * u
                    u = lam * (u + lt[l, L_Q, t] * x[t])
    return sums


def explicit(r, l, t, before, here, after, ext_here, ext_diff, ml, kl, qs, xs):
    here = [here(k) for k in range(KT)]
    around = []
    diff = []
    for k in range(KT):
        up, down = before(k), after(k)
        around.append(down + up - 2.0 * here[k])
        diff.append(down - up)
    flat = zip(turned(lambda k: here[k], ext_here), turned(lambda k: diff[k], ext_diff))
    for k, ((east, west), (diff_east, diff_west)) in enumerate(flat):
        lon = east + west - 2.0 * here[k]
        inner = here[k] + ml[l, k, t] * (diff_east - diff_west) + (2.0 * r.a1) * lon + (2.0 * r.a2) * around[k]
        qs[l, k, t] = kl[k, t] * inner - r.a1 * lon
        xs[l, k, t] = -r.a2 * around[k]


def end_columns(first, last):
    lane = iota((ROWS, LN), 1)
    turned = jnp.where(lane < 64, first, last).T
    return turned[0:1], turned[LN - 1 : LN]


def first_kernel(par, ul, ml, kl, north, south, wt, kt, et, lt, zl, phi, msg, uh, kh, qs, xs, ss):
    def spread(ref, row):
        return jnp.stack([jnp.broadcast_to(ref[row, k : k + 1, :], (SS, LN)) for k in range(KT)])

    for side, ref in ((0, north), (1, south)):
        kh[side, :KT] = spread(ref, 2)
    for l in range(LEV):
        r = Rates(par, l)
        uh[l, 0, :KT] = spread(north, l)
        uh[l, 1, :KT] = spread(south, l)

        for t in range(TT):
            if t == 0:
                before = lambda k: north_of(ul[l, k, TT - 1], uh[l, 0, k])
            else:
                before = lambda k, t=t: ul[l, k, t - 1]
            if t == TT - 1:
                after = lambda k: south_of(ul[l, k, 0], uh[l, 1, k])
            else:
                after = lambda k, t=t: ul[l, k, t + 1]
            explicit(r, l, t, before, lambda k, t=t: ul[l, k, t], after, None, None, ml, kl, qs, xs)
    sums = local_solve(par, qs, xs, ss, wt, kt, et, lt, zl, phi, True)
    parts = []
    for l in range(LEV):
        parts.append(sums[l].T[96:98])
    for l in range(LEV):
        parts.extend(end_columns(ul[l, 0].reshape(ROWS, LN), ul[l, KT - 1].reshape(ROWS, LN)))
    for l in range(LEV):
        parts.extend(end_columns(ml[l, 0].reshape(ROWS, LN), ml[l, KT - 1].reshape(ROWS, LN)))
    parts.extend(end_columns(kl[0].reshape(ROWS, LN), kl[KT - 1].reshape(ROWS, LN)))
    lane = iota((1, LN), 1)
    for row in range(3):
        n0, s0 = north[row, 0:1, :], south[row, 0:1, :]
        n1, s1 = north[row, KT - 1 : KT, :], south[row, KT - 1 : KT, :]
        parts.append(jnp.where(lane == 0, n0, pltpu.roll(s0, 1, 1)))
        parts.append(jnp.where(lane == LN - 1, n1, pltpu.roll(s1, LN - 1, 1)))
    parts.append(jnp.zeros((4, LN), F32))
    block = jnp.concatenate(parts, axis=0)
    for j in range(NLON_DEV):
        msg[j] = block


def row_after(x, halo):
    lane = iota(x.shape, 1)
    y = jnp.where(lane >= LN - SS, pltpu.roll(x, LN - SS - 1, 1), pltpu.roll(x, LN - SS, 1))
    return jnp.where(lane == LN - 1, halo, y)


def row_before(x, halo):
    lane = iota(x.shape, 1)
    y = jnp.where(lane < SS, pltpu.roll(x, SS + 1, 1), pltpu.roll(x, SS, 1))
    return jnp.where(lane == 0, halo, y)


def lane_value(x, index):
    return jnp.sum(jnp.where(iota(x.shape, x.ndim - 1) == index, x, 0.0), axis=-1, keepdims=True)


def as_tile(rows):
    count = sum(r.shape[0] for r in rows)
    return jnp.concatenate(rows + [jnp.zeros((LN - count, LN), F32)], axis=0).T.reshape(TT, SS, LN)


def carry_kernel(first, *refs):
    if first:
        par, got, phi, lt, el, out, pack, ze, ux, kx, uhx, khx = refs
    else:
        par, got, phi, px, lt, el, out, pack, ze = refs
    i_pos, j_pos = position()
    peer = fiota((NLON_DEV, LN), 0)
    mine = peer == j_pos
    fluxes = []
    ext = []
    if first:
        kw = pltpu.roll(got[:, 13, :], 1, 0)
        ke = pltpu.roll(got[:, 12, :], NLON_DEV - 1, 0)
        kw_end = pltpu.roll(got[:, 19, :], 1, 0)
        ke_end = pltpu.roll(got[:, 18, :], NLON_DEV - 1, 0)

        def own(x):
            return jnp.sum(jnp.where(mine, x, 0.0), axis=0, keepdims=True)

        def corners(west_end, east_end):
            lane = iota((1, LN), 1)
            w, e = own(west_end), own(east_end)
            w_n, w_s = lane_value(w, LN - 1), lane_value(w, LN - 2)
            e_n, e_s = lane_value(e, 0), lane_value(e, 1)
            pick = lambda a, b: jnp.broadcast_to(jnp.where(lane == 0, a, jnp.where(lane == 1, b, 0.0)), (SS, LN))
            return pick(w_n, e_n), pick(w_s, e_s)

        khx[0], khx[1] = corners(kw_end, ke_end)
        kx[...] = as_tile([own(kw), own(ke)])
    for l in range(LEV):
        r = Rates(par, l)
        a, b = got[:, 2 * l, :], got[:, 2 * l + 1, :]
        one = jnp.full((NLON_DEV, LN), 1.0, F32)
        if first:
            uw = pltpu.roll(got[:, 5 + 2 * l, :], 1, 0)
            ue = pltpu.roll(got[:, 4 + 2 * l, :], NLON_DEV - 1, 0)
            uw_end = pltpu.roll(got[:, 15 + 2 * l, :], 1, 0)
            ue_end = pltpu.roll(got[:, 14 + 2 * l, :], NLON_DEV - 1, 0)
            w_up = row_before(uw, jnp.sum(jnp.where(iota(uw.shape, 1) == LN - 1, uw_end, 0.0), axis=1, keepdims=True))
            w_dn = row_after(uw, jnp.sum(jnp.where(iota(uw.shape, 1) == LN - 2, uw_end, 0.0), axis=1, keepdims=True))
            e_up = row_before(ue, jnp.sum(jnp.where(iota(ue.shape, 1) == 0, ue_end, 0.0), axis=1, keepdims=True))
            e_dn = row_after(ue, jnp.sum(jnp.where(iota(ue.shape, 1) == 1, ue_end, 0.0), axis=1, keepdims=True))
            m0, mn, k0, kn = got[:, 8 + 2 * l, :], got[:, 9 + 2 * l, :], got[:, 12, :], got[:, 13, :]
            h0 = k0 * (m0 * (w_up - w_dn) + 2.0 * r.a1 * uw) - r.a1 * uw
            hn = kn * (mn * (e_dn - e_up) + 2.0 * r.a1 * ue) - r.a1 * ue
            far = jnp.exp(-(COLS - 1.0) * r.t1 * one)
            a = a + far * h0 + hn
            b = b + h0 + far * hn
        whole = 1.0 - jnp.exp(-float(NLON) * r.t1 * one)
        back = j_pos - peer - 1.0
        back = jnp.where(back < 0, back + NLON_DEV, back)
        ahead = peer - j_pos - 1.0
        ahead = jnp.where(ahead < 0, ahead + NLON_DEV, ahead)
        left = jnp.sum(a * (jnp.exp(-r.t1 * COLS * back) / whole), axis=0, keepdims=True)
        right = jnp.sum(b * (jnp.exp(-r.t1 * COLS * ahead) / whole), axis=0, keepdims=True)
        a = jnp.sum(jnp.where(mine, a, 0.0), axis=0, keepdims=True)
        b = jnp.sum(jnp.where(mine, b, 0.0), axis=0, keepdims=True)
        lam = jnp.exp(-r.t1 * jnp.full((1, LN), 1.0, F32))
        far = jnp.exp(-(COLS + 1.0) * r.t1 * jnp.full((1, LN), 1.0, F32))
        xw = r.c1 * (left + lam * b + far * right)
        xe = r.c1 * (right + lam * a + far * left)
        if first:
            pw = -r.a2 * (w_dn + w_up - 2.0 * uw)
            pe = -r.a2 * (e_dn + e_up - 2.0 * ue)
            xw = xw + own(pw)
            xe = xe + own(pe)
            left = left + own(h0) / lam
            right = right + own(hn) / lam
            ux[l] = as_tile([own(uw), own(ue)])
            uhx[l, 0], uhx[l, 1] = corners(uw_end, ue_end)
        x = as_tile([xw, xe, left, right])
        if not first:
            x = x + px[l]
        ext.append(x)
    lams = [lam2(Rates(par, l).t2) for l in range(LEV)]
    zero = jnp.zeros((SS, LN), F32)
    state = [zero, zero]
    acc = [zero, zero]
    kept = [[], []]
    for t in range(TT):
        for l in range(LEV):
            state[l] = lams[l] * state[l] + lt[l, L_P, t] * ext[l][t]
            acc[l] = acc[l] + lt[l, L_LQ, t] * ext[l][t]
            kept[l].append(state[l])
    for l in range(LEV):
        r = Rates(par, l)
        carry_down, carry_up, phi_e, psi_e = chunk_ends(state[l], acc[l], r.t2)
        u = lams[l] * carry_up
        for t in range(TT - 1, -1, -1):
            ze[l, t] = lt[l, L_CQ, t] * kept[l][t] + lt[l, L_CQL, t] * carry_down + lt[l, L_CP, t] * u
            u = lams[l] * (u + lt[l, L_Q, t] * ext[l][t])
        pair = []
        for side, flux in ((0, phi_e), (1, psi_e)):
            tiles = phi[l, side] + lane_value(flux, 2) * el[l, 0] + lane_value(flux, 3) * el[l, 1]
            pair.append([tiles[k] for k in range(KT)] + [flux])
        fluxes.append(pair)
    sub = iota((SS, LN), 0)
    packed = []
    for side in (0, 1):
        rows = fluxes[0][side] + fluxes[1][side]
        rows = rows + [zero] * (PK - len(rows))
        vregs = []
        for v in range(PK // SS):
            y = rows[v * SS]
            for j in range(1, SS):
                y = jnp.where(sub == j, rows[v * SS + j], y)
            vregs.append(y)
        packed.append(jnp.concatenate(vregs, axis=0))
        pack[side] = packed[side]
    t2 = level_rows(Rates(par, 0).t2, Rates(par, 1).t2)
    for p in range(NLAT_DEV):
        away = jnp.maximum(jnp.abs(p - i_pos) - 1.0, 0.0)
        factor = jnp.exp(-(ROWS * away) * t2)
        ahead = jnp.full((PK, LN), p - i_pos, F32) > 0
        out[p] = factor * jnp.where(ahead, packed[0], packed[1])


def level_rows(low, high):
    return jnp.where(iota((PK, LN), 0) <= KT, low, high)


def arrive(par, got, pack, tb, vb, hb):
    i_pos, _ = position()
    zero = jnp.zeros((PK, LN), F32)
    above, below = zero, zero
    for p in range(NLAT_DEV):
        side = jnp.full((PK, LN), p - i_pos, F32)
        above = above + jnp.where(side < 0, got[p], 0.0)
        below = below + jnp.where(side > 0, got[p], 0.0)
    t2 = level_rows(Rates(par, 0).t2, Rates(par, 1).t2)
    scale = level_rows(Rates(par, 0).c2, Rates(par, 1).c2) / (1.0 - jnp.exp(-2.0 * (NLAT + 1) * t2))
    lam = jnp.exp(-t2)
    block = jnp.exp(-float(ROWS) * t2)
    start = i_pos * ROWS
    q_n = 1.0 - jnp.exp(-2.0 * t2 * (NLAT + 1.0 - start))
    p_n = 1.0 - jnp.exp(-2.0 * t2 * start)
    q_s = 1.0 - jnp.exp(-2.0 * t2 * (NLAT - ROWS - start))
    p_s = 1.0 - jnp.exp(-2.0 * t2 * (ROWS + 1.0 + start))
    north = scale * (q_n * above + p_n * lam * (pack[1] + block * below))
    south = scale * (q_s * lam * (pack[0] + block * above) + p_s * below)
    for l in range(LEV):
        for k in range(KT + 1):
            at = l * (KT + 1) + k
            wide = lambda x: jnp.broadcast_to(x[at : at + 1], (SS, LN))
            tb[l, k] = wide(above)
            vb[l, k] = wide(below)
            if hb is not None:
                hb[l, 0, k] = wide(north)
                hb[l, 1, k] = wide(south)


def solved_rows(l, zl, ze, el, lt, tb, vb, use, use_extra):
    step = 4
    for start in range(0, TT, step):
        times = range(start, start + step)
        extra = [ze[l, t] for t in times]
        gq = [lt[l, L_GQ, t] for t in times]
        gp = [lt[l, L_GP, t] for t in times]
        z_left = [jnp.broadcast_to(x[:, 2:3], (SS, LN)) for x in extra]
        z_right = [jnp.broadcast_to(x[:, 3:4], (SS, LN)) for x in extra]
        for k in range(KT):
            e_left, e_right, above, below = el[l, 0, k], el[l, 1, k], tb[l, k], vb[l, k]
            for i, t in enumerate(times):
                use(k, t, zl[l, k, t] + e_left * z_left[i] + e_right * z_right[i] + gq[i] * above + gp[i] * below)
        if use_extra is not None:
            above, below = tb[l, KT], vb[l, KT]
            for i, t in enumerate(times):
                use_extra(t, extra[i] + gq[i] * above + gp[i] * below)


def send_sums(sums, msg):
    block = jnp.concatenate([s.T[96:98] for s in sums] + [jnp.zeros((4, LN), F32)], axis=0)
    for j in range(NLON_DEV):
        msg[j] = block


def half_kernel(par, got, pack, zl, ze, ul, ux, uh, uhx, ml, el, wt, kt, et, lt,
                y2, yx, yh, zo, phi, msg, px, tb, vb, vs, qs, xs, ss):
    arrive(par, got, pack, tb, vb, yh)
    for l in range(LEV):
        r = Rates(par, l)

        def use(k, t, own):
            y2[l, k, t] = own
            vs[k, t + 1] = own - ul[l, k, t]

        def use_extra(t, extra):
            yx[l, t] = extra
            vs[KT, t + 1] = extra - ux[l, t]
            px[l, t] = jnp.zeros((SS, LN), F32)

        solved_rows(l, zl, ze, el, lt, tb, vb, use, use_extra)
        for side, edge, at, turn in ((0, TT, 0, north_of), (1, 1, TT + 1, south_of)):
            vs[:KT, at] = turn(vs[:KT, edge], yh[l, side, :KT] - uh[l, side, :KT])
            vs[KT, at] = turn(vs[KT, edge], yh[l, side, KT] - uhx[l, side])

        for t in range(TT):
            diff = [vs[k, t + 2] - vs[k, t] for k in range(KT + 1)]
            for k, (east, west) in enumerate(turned(lambda k: diff[k], diff[KT])):
                qs[l, k, t] = 0.5 * ml[l, k, t] * (east - west)
    send_sums(local_solve(par, qs, xs, ss, wt, kt, et, lt, zo, phi, False), msg)


def step_kernel(par, got, pack, zl, ze, y2, yx, yh, kl, kx, kh, khx, ml, el, wt, kt, et, lt,
                un, unx, unh, unhx, zo, phi, msg, px, tb, vb, hb, vs, qs, xs, ss):
    arrive(par, got, pack, tb, vb, hb)
    for l in range(LEV):
        r = Rates(par, l)

        def use(k, t, own):
            own = kl[k, t] * (own + y2[l, k, t])
            un[l, k, t] = own
            vs[k, t + 1] = own

        def use_extra(t, extra):
            extra = kx[t] * (extra + yx[l, t])
            unx[l, t] = extra
            vs[KT, t + 1] = extra

        solved_rows(l, zl, ze, el, lt, tb, vb, use, use_extra)
        for side, edge, at, turn in ((0, TT, 0, north_of), (1, 1, TT + 1, south_of)):
            halo = kh[side, :KT] * (yh[l, side, :KT] + hb[l, side, :KT])
            halo_x = khx[side] * (yh[l, side, KT] + hb[l, side, KT])
            unh[l, side, :KT] = halo
            unhx[l, side] = halo_x
            vs[:KT, at] = turn(vs[:KT, edge], halo)
            vs[KT, at] = turn(vs[KT, edge], halo_x)

        for t in range(TT):
            before, here, after = vs[KT, t], vs[KT, t + 1], vs[KT, t + 2]
            explicit(r, l, t, lambda k: vs[k, t], lambda k: vs[k, t + 1], lambda k: vs[k, t + 2],
                     here, after - before, ml, kl, qs, xs)
            px[l, t] = jnp.where(iota((SS, LN), 1) < 2, -r.a2 * (after + before - 2.0 * here), 0.0)
    send_sums(local_solve(par, qs, xs, ss, wt, kt, et, lt, zo, phi, True), msg)


def last_kernel(par, got, pack, zl, ze, y2, kl, el, lt, out, tb, vb, zs, os, sem):
    arrive(par, got, pack, tb, vb, None)
    copies = []
    for l in range(LEV):
        for k in range(KT):
            e_left, e_right, above, below = el[l, 0, k], el[l, 1, k], tb[l, k], vb[l, k]
            for t in range(TT):
                if k == 0:
                    extra = ze[l, t]
                    zs[0, t] = jnp.broadcast_to(extra[:, 2:3], (SS, LN))
                    zs[1, t] = jnp.broadcast_to(extra[:, 3:4], (SS, LN))
                z = zl[l, k, t] + e_left * zs[0, t] + e_right * zs[1, t]
                z = z + lt[l, L_GQ, t] * above + lt[l, L_GP, t] * below
                os[l, k, pl.ds(t, SS, stride=TT), :] = kl[k, t] * (z + y2[l, k, t])
            copies.append(pltpu.make_async_copy(os.at[l, k], out.at[l, :, pl.ds(k * LN, LN)], sem.at[l]))
            copies[-1].start()
    for c in copies:
        c.wait()


FIELD = (LEV, KT, TT, SS, LN)
EXTRA = (LEV, TT, SS, LN)
HALO = (LEV, 2, KT + 1, SS, LN)
FLUX = (LEV, 2, KT, SS, LN)


def call(kernel, outs, ins, scratch=(), out_specs=None, in_specs=None, limit=10):
    return pl.pallas_call(
        kernel,
        out_shape=outs,
        in_specs=in_specs or [SM] + [VM] * (len(ins) - 1),
        out_specs=out_specs or [VM] * len(outs),
        scratch_shapes=list(scratch),
        compiler_params=pltpu.CompilerParams(vmem_limit_bytes=limit * 1024 * 1024),
    )(*ins)


def vmem(*dims):
    return pltpu.VMEM(dims, F32)


def rows_kernel(u_hbm, k_hbm, one, two, su, sk, sem):
    copies = []
    for side, at in ((0, 0), (1, ROWS - SS)):
        for l in range(LEV):
            copies.append(pltpu.make_async_copy(u_hbm.at[l, pl.ds(at, SS)], su.at[l, side], sem.at[l, side]))
        copies.append(pltpu.make_async_copy(k_hbm.at[pl.ds(at, SS)], sk.at[side], sem.at[LEV, side]))
    for c in copies:
        c.start()
    for c in copies:
        c.wait()
    even = jnp.full((1, LN), lax.axis_index("lat") % 2, jnp.int32) == 0
    for k in range(KT):
        at = pl.ds(k * LN, LN)
        for row in range(LEV + 1):
            if row < LEV:
                first, last = su[row, 0, 0:1, at], su[row, 1, SS - 1 : SS, at]
            else:
                first, last = sk[0, 0:1, at].astype(F32), sk[1, SS - 1 : SS, at].astype(F32)
            one[row, k : k + 1, :] = jnp.where(even, last, first)
            two[row, k : k + 1, :] = jnp.where(even, first, last)


def halo_rows(ensemble, mask):
    one, two = call(
        rows_kernel,
        [shape(LEV + 1, KT, LN), shape(LEV + 1, KT, LN)],
        [ensemble[:, 0], mask],
        [vmem(LEV, 2, SS, COLS), pltpu.VMEM((2, SS, COLS), jnp.int32), pltpu.SemaphoreType.DMA((LEV + 1, 2))],
        in_specs=[HB, HB],
        limit=57,
    )
    pairs = [(i, i + 1) for i in range(0, NLAT_DEV, 2)]
    odd_pairs = [(i, i + 1) for i in range(1, NLAT_DEV - 1, 2)]
    both = lambda edges: edges + [(j, i) for i, j in edges]
    one = lax.ppermute(one, "lat", both(pairs))
    two = lax.ppermute(two, "lat", both(odd_pairs))
    even = lax.axis_index("lat") % 2 == 0
    return jnp.where(even, two, one), jnp.where(even, one, two)


def exchange(values, axis):
    return lax.all_to_all(values, axis, split_axis=0, concat_axis=0, tiled=True)


def shards(ensemble, cross_mix, sea_mask, level_rates, panel_inverse, reduced_lon, reduced_lat):
    par = level_rates
    north, south = halo_rows(ensemble, sea_mask)
    work = [vmem(*FIELD), vmem(*FIELD), vmem(KT, TT, SS, LN)]
    carries = [vmem(LEV, KT + 1, SS, LN), vmem(LEV, KT + 1, SS, LN)]
    diffs = vmem(KT + 1, TT + 2, SS, LN)
    ul, ml, kl, done = call(
        move_kernel,
        [shape(*FIELD), shape(*FIELD), shape(KT, TT, SS, LN), shape(SS, LN)],
        [ensemble[:, 0], cross_mix, sea_mask],
        [vmem(LEV, KT, ROWS, LN), vmem(LEV, KT, ROWS, LN), pltpu.VMEM((KT, ROWS, LN), jnp.int32),
         pltpu.SemaphoreType.DMA((5,))],
        in_specs=[HB, HB, HB],
        limit=45,
    )
    wt, kt, et, lt, el = call(
        tables_kernel,
        [shape(LEV, KT, 3, LN, LN, dtype=BF16), shape(LEV, 3, LN, LN, dtype=BF16),
         shape(LEV, 2 * LN, COLS, dtype=BF16), shape(LEV, 8, TT, SS, LN), shape(LEV, 2, KT, SS, LN)],
        [par, done],
    )
    mats = [wt, kt, et, lt]
    solve_out = [shape(*FIELD), shape(*FLUX), shape(NLON_DEV, 8, LN)]
    carry_out = [shape(NLAT_DEV, PK, LN), shape(2, PK, LN), shape(*EXTRA)]
    zl, phi, msg, uh, kh = call(
        first_kernel,
        [shape(*FIELD), shape(*FLUX), shape(NLON_DEV, 24, LN), shape(*HALO), shape(2, KT + 1, SS, LN)],
        [par, ul, ml, kl, north, south] + mats,
        work,
    )
    got = exchange(msg, "lon")
    out, pack, ze, ux, kx, uhx, khx = call(
        functools.partial(carry_kernel, True),
        carry_out + [shape(*EXTRA), shape(TT, SS, LN), shape(LEV, 2, SS, LN), shape(2, SS, LN)],
        [par, got, phi, lt, el],
    )
    for step in range(2):
        got = exchange(out, "lat")
        y2, yx, yh, zl, phi, msg, px = call(
            half_kernel,
            [shape(*FIELD), shape(*EXTRA), shape(*HALO)] + solve_out + [shape(*EXTRA)],
            [par, got, pack, zl, ze, ul, ux, uh, uhx, ml, el] + mats,
            carries + [diffs] + work,
        )
        got = exchange(msg, "lon")
        out, pack, ze = call(functools.partial(carry_kernel, False), carry_out, [par, got, phi, px, lt, el])
        got = exchange(out, "lat")
        if step == 1:
            break
        ul, ux, uh, uhx, zl, phi, msg, px = call(
            step_kernel,
            [shape(*FIELD), shape(*EXTRA), shape(*HALO), shape(LEV, 2, SS, LN)] + solve_out + [shape(*EXTRA)],
            [par, got, pack, zl, ze, y2, yx, yh, kl, kx, kh, khx, ml, el] + mats,
            carries + [vmem(*HALO), diffs] + work,
        )
        got = exchange(msg, "lon")
        out, pack, ze = call(functools.partial(carry_kernel, False), carry_out, [par, got, phi, px, lt, el])
    (final,) = call(
        last_kernel,
        [shape(LEV, ROWS, COLS)],
        [par, got, pack, zl, ze, y2, kl, el, lt],
        carries + [vmem(2, TT, SS, LN), vmem(LEV, KT, ROWS, LN), pltpu.SemaphoreType.DMA((LEV,))],
        out_specs=[HB],
    )
    return final[:, None]


def solution(mesh):
    in_specs = (
        P(None, None, "lat", "lon"),
        P(None, "lat", "lon"),
        P("lat", "lon"),
        P(),
        P(),
        P(),
        P(),
    )
    out_specs = P(None, None, "lat", "lon")
    return jax.shard_map(shards, mesh=mesh, in_specs=in_specs, out_specs=out_specs, check_vma=False)
```
